128 devices in a mesh: seq: 32 (over y, x_hi, z), chan: 4 (over x_lo, core).
Axes of the slice: x: 4 (x_hi: 2, x_lo: 2; x = x_hi * 2 + x_lo), y: 4, z: 4, core: 2. Of those that a mesh axis runs over, the one named last changes fastest.
Arguments:
- inputs: bfloat16 [256, 512, 1536], P('seq', None, 'chan'), may hold values from -6 to 6
- gate_values: bfloat16 [256, 512, 1536], P('seq', None, 'chan'), may hold values from -6 to 6
- kernel: bfloat16 [256, 512, 1536], P('seq', None, 'chan'), may hold values from -6 to 6
- grad_out: bfloat16 [512, 256, 1536], P('seq', None, 'chan'), may hold values from -6 to 6
- left_tiles: bfloat16 [256, 8, 256], P(('seq', 'chan')), may hold values from -0.375 to 0.375
- right_tiles: bfloat16 [512, 8, 512], P(('seq', 'chan')), may hold values from -0.25 to 0.25
Outputs:
- output: bfloat16 [512, 256, 1536], P('seq', None, 'chan')
- grad_inputs: bfloat16 [256, 512, 1536], P('seq', None, 'chan')
- grad_gates: bfloat16 [256, 512, 1536], P('seq', None, 'chan')
- grad_kernel: bfloat16 [256, 512, 1536], P('seq', None, 'chan')
- grad_left: float32 [256, 8, 256], P(('seq', 'chan'))
- grad_right: float32 [512, 8, 512], P(('seq', 'chan'))
The draws below stay inside these ranges and needn't reach their ends.
All inputs are finite; a program needn't handle non-finite values.
Results may differ from the reference program's by a relative error of at most 0.0058.
Values may be sent and summed in bfloat16 or wider, within the bound.
A program may use at most 192 MiB of HBM per device.

```python
import math
import jax
import jax.numpy as jnp
from jax import lax

A = 256
B = 512
C = 1536
H = 8


def level_of(key, shape, split, least, high):
    def one(position, parts):
        heights = jax.random.uniform(jax.random.fold_in(jax.random.fold_in(key, 6), position), (parts,), jnp.float32, least / len(split), high / len(split))
        return jnp.repeat(jnp.exp(heights), shape[position] // parts).reshape((-1,) + (1,) * (len(shape) - position - 1))

    level = one(*split[0])
    for cut in split[1:]:
        level = level * one(*cut)
    return level


def gaussian(key, shape, width, most, shards=(), kind=jnp.bfloat16):
    entries = jax.random.normal(key, shape, jnp.float32) * width
    if len(shards) > 0:
        entries = level_of(key, shape, shards, -0.22, 0.18) * entries
    return jnp.clip(entries, min=-most, max=most).astype(kind)


def setup_inputs(seed: int = 0) -> dict:
    seeds = jax.random.split(jax.random.key(seed), 7)
    inputs = gaussian(seeds[0], (A, B, C), 1.0, 6.0, ((0, 32), (2, 4)))
    gate_values = gaussian(seeds[1], (A, B, C), 1.0, 6.0, ((0, 32), (2, 4)))
    kernel = gaussian(seeds[2], (A, B, C), 1.0, 6.0, ((0, 32), (2, 4)))
    grad_out = gaussian(seeds[3], (B, A, C), 1.0, 6.0, ((0, 32), (2, 4)))
    left_tiles = gaussian(seeds[4], (A, H, A), A ** -0.5, 0.375, ((0, 128),))
    right_tiles = gaussian(seeds[5], (B, H, B), B ** -0.5, 0.25, ((0, 128),))
    return dict(inputs=inputs, gate_values=gate_values, kernel=kernel, grad_out=grad_out, left_tiles=left_tiles, right_tiles=right_tiles)


def reference(inputs, gate_values, kernel, grad_out, left_tiles, right_tiles):
    depth = C // H
    right = right_tiles.astype(jnp.float32)
    left = left_tiles.astype(jnp.float32)

    def inner_product(row_in, row_gate):
        gated = (row_in.astype(jnp.float32) * row_gate.astype(jnp.float32)).astype(jnp.bfloat16)
        gated_three = gated.astype(jnp.float32).reshape(B, depth, H)
        spectral = jnp.einsum('phb,bdh->pdh', right, gated_three).reshape(B, C)
        return (gated_three, spectral)

    def forward_row(row_args):
        row_in, row_gate, row_kernel = row_args
        gated_three, spectral = inner_product(row_in, row_gate)
        return (row_kernel.astype(jnp.float32) * spectral).astype(jnp.bfloat16)
    twisted = lax.map(forward_row, (inputs, gate_values, kernel))
    turned = jnp.swapaxes(twisted, 0, 1)

    def column_step(summed, col_args):
        twist_col, grad_col = col_args
        twist_three = twist_col.astype(jnp.float32).reshape(A, depth, H)
        grad_three = grad_col.astype(jnp.float32).reshape(A, depth, H)
        mixed = jnp.einsum('qha,adh->qdh', left, twist_three).reshape(A, C).astype(jnp.bfloat16)
        back_col = jnp.einsum('qha,qdh->adh', left, grad_three).reshape(A, C).astype(jnp.bfloat16)
        summed = summed + jnp.einsum('qdh,adh->qha', grad_three, twist_three)
        return (summed, (mixed, back_col))
    grad_left, (output, back_cols) = lax.scan(column_step, jnp.zeros((A, H, A), jnp.float32), (turned, grad_out))
    back_twist = jnp.swapaxes(back_cols, 0, 1)

    def row_step(summed, row_args):
        row_in, row_gate, row_kernel, row_back = row_args
        gated_three, spectral = inner_product(row_in, row_gate)
        back_f = row_back.astype(jnp.float32)
        grad_kern = (back_f * spectral).astype(jnp.bfloat16)
        pushed = (row_kernel.astype(jnp.float32) * back_f).astype(jnp.bfloat16)
        pushed_three = pushed.astype(jnp.float32).reshape(B, depth, H)
        grad_gated = jnp.einsum('phb,pdh->bdh', right, pushed_three).reshape(B, C)
        grad_in = (grad_gated * row_gate.astype(jnp.float32)).astype(jnp.bfloat16)
        grad_gate = (grad_gated * row_in.astype(jnp.float32)).astype(jnp.bfloat16)
        summed = summed + jnp.einsum('pdh,bdh->phb', pushed_three, gated_three)
        return (summed, (grad_in, grad_gate, grad_kern))
    grad_right, (grad_inputs, grad_gates, grad_kernel) = lax.scan(row_step, jnp.zeros((B, H, B), jnp.float32), (inputs, gate_values, kernel, back_twist))
    grad_left = grad_left / math.sqrt(B * C / H)
    grad_right = grad_right / math.sqrt(A * C / H)
    return (output, grad_inputs, grad_gates, grad_kernel, grad_left, grad_right)
```

```python
import functools
import math

import jax
import jax.numpy as jnp
from jax import lax
from jax.experimental import pallas as pl
from jax.experimental.pallas import tpu as pltpu
from jax.sharding import PartitionSpec as P

MESH = pl.DeviceIdType.MESH
BF = jnp.bfloat16
F32 = jnp.float32
A = 256
B = 512
C = 1536
H = 8
LANE = 128
SEQ = 32
RIGHT_PARTS = ((0, 32, (0, 1, 2)), (32, 16, (1, 2, 0)), (48, 16, (2, 0, 1)))
LEFT_PARTS = ((0, 32, (2, 0, 1)),)


def place():
    seq = lax.axis_index("seq")
    chan = lax.axis_index("chan")
    x = ((seq // 4) % 2) * 2 + chan // 2
    return (x, seq // 8, seq % 4), chan % 2


def device_at(xyz, core):
    x, y, z = xyz
    return (y * 8 + (x // 2) * 4 + z, (x % 2) * 2 + core)


def moved(xyz, axis, step):
    new = list(xyz)
    new[axis] = (xyz[axis] + step) % 4
    return tuple(new)


def greet(devices):
    barrier = pltpu.get_barrier_semaphore()
    for device in devices:
        pl.semaphore_signal(barrier, inc=1, device_id=device, device_id_type=MESH)
    pl.semaphore_wait(barrier, len(devices))


def chip_friends(xyz, core):
    return [device_at(xyz, 1 - core)] + [
        device_at(moved(xyz, axis, step), core) for axis in range(3) for step in (1, 2, 3)
    ]


def remote(src, dst, send, recv, device):
    return pltpu.make_async_remote_copy(
        src_ref=src, dst_ref=dst, send_sem=send, recv_sem=recv, device_id=device, device_id_type=MESH
    )


def aligned(value, multiple):
    return pl.multiple_of(value, multiple)


def gather_kernel(right_ref, left_ref, right_out, left_out, raw_r, raw_l, piece, local_sem, core_sems, axis_sems):
    xyz, core = place()
    x, y, z = xyz
    sibling = device_at(xyz, 1 - core)
    greet(chip_friends(xyz, core))
    half_r = pl.ds(aligned(core * 256, 256), 256)
    half_l = pl.ds(aligned(core * 128, 128), 128)
    other_r = pl.ds(aligned((1 - core) * 256, 256), 256)
    other_l = pl.ds(aligned((1 - core) * 128, 128), 128)
    rows_r = pl.ds(aligned(core * 32, 32), 32)
    rows_l = pl.ds(aligned(core * 16, 16), 16)
    first = [
        remote(right_ref.at[:, other_r], raw_r.at[x, y, z, rows_r, other_r], core_sems.at[0, 0], core_sems.at[1, 0], sibling),
        remote(left_ref.at[:, other_l], raw_l.at[x, y, z, rows_l, other_l], core_sems.at[0, 1], core_sems.at[1, 1], sibling),
    ]
    for copy in first:
        copy.start()
    own = [
        pltpu.make_async_copy(right_ref.at[:, half_r], raw_r.at[x, y, z, rows_r, half_r], local_sem.at[0]),
        pltpu.make_async_copy(left_ref.at[:, half_l], raw_l.at[x, y, z, rows_l, half_l], local_sem.at[1]),
    ]
    for copy in own:
        copy.start()
    for copy in own:
        copy.wait()
    for copy in first:
        copy.wait()
    parts = [(raw_l, half_l) + part for part in LEFT_PARTS] + [(raw_r, half_r) + part for part in RIGHT_PARTS]
    stages = {}
    for stage in range(4):
        for number, (buf, half, row, rows, order) in enumerate(parts):
            if stage > 0:
                for copy in stages[number]:
                    copy.wait()
            if stage == 3:
                continue
            index = tuple(slice(None) if axis in order[:stage] else xyz[axis] for axis in range(3))
            ref = buf.at[index + (pl.ds(row, rows), half)]
            stages[number] = [
                remote(
                    ref,
                    ref,
                    axis_sems.at[0, number, stage, step - 1],
                    axis_sems.at[1, number, stage, step - 1],
                    device_at(moved(xyz, order[stage], step), core),
                )
                for step in (1, 2, 3)
            ]
            for copy in stages[number]:
                copy.start()
    mine = [raw_l.at[:, :, :, :, half_l], raw_r.at[:, :, :, :, half_r]]
    last = [
        remote(ref, ref, core_sems.at[0, 2 + n], core_sems.at[1, 2 + n], sibling) for n, ref in enumerate(mine)
    ]
    for copy in last:
        copy.start()
    for copy in last:
        copy.wait()

    def right_rows(seq, _):
        cy, cx, cz = seq // 8, (seq // 4) % 2, seq % 4
        for lane in range(4):
            lanes = slice(lane * LANE, (lane + 1) * LANE)
            for lo in range(2):
                piece[lane, lo * 64 : lo * 64 + 64, :] = raw_r[cx * 2 + lo, cy, cz, :, lanes].astype(F32)
            for h in range(H):
                right_out[h, pl.ds(aligned(seq * 16, 16), 16), lanes] = piece[lane, pl.ds(h, 16, stride=8), :].astype(BF)
        return _

    def left_rows(pair, _):
        seq = pair * 2
        cy, cx, cz = seq // 8, (seq // 4) % 2, seq % 4
        for lane in range(2):
            lanes = slice(lane * LANE, (lane + 1) * LANE)
            for n in range(4):
                piece[lane, n * 32 : n * 32 + 32, :] = raw_l[cx * 2 + n % 2, cy, cz + n // 2, :, lanes].astype(F32)
            for h in range(H):
                left_out[h, pl.ds(aligned(pair * 16, 16), 16), lanes] = piece[lane, pl.ds(h, 16, stride=8), :].astype(BF)
        return _

    lax.fori_loop(0, 16, left_rows, 0)
    lax.fori_loop(0, 32, right_rows, 0)


def gather_tiles(right, left):
    vmem = pl.BlockSpec(memory_space=pltpu.VMEM)
    return pl.pallas_call(
        gather_kernel,
        out_shape=(jax.ShapeDtypeStruct((H, B, B), BF), jax.ShapeDtypeStruct((H, A, A), BF)),
        in_specs=[vmem, vmem],
        out_specs=(vmem, vmem),
        scratch_shapes=[
            pltpu.VMEM((4, 4, 4, 64, 512), BF),
            pltpu.VMEM((4, 4, 4, 32, 256), BF),
            pltpu.VMEM((4, 128, LANE), F32),
            pltpu.SemaphoreType.DMA((2,)),
            pltpu.SemaphoreType.DMA((2, 4)),
            pltpu.SemaphoreType.DMA((2, 4, 3, 3)),
        ],
        compiler_params=pltpu.CompilerParams(collective_id=0, has_side_effects=True, vmem_limit_bytes=40 << 20),
        name="gather_tiles",
    )(right, left)


def masks_of(rows):
    lane = lax.broadcasted_iota(jnp.int32, (rows, LANE), 1)
    return [(lane & bit) != 0 for bit in (1, 2, 4)]


def turn(values, masks):
    for bit, mask in zip((1, 2, 4), masks):
        values = [jnp.where(mask, values[(i + bit) % 8], values[i]) for i in range(8)]
    return values


def to_groups(values, masks):
    values = turn([v if n == 0 else pltpu.roll(v, n, 1) for n, v in enumerate(values)], masks)
    return [values[(-h) % 8] for h in range(8)]


def from_groups(values, masks):
    values = turn(values, masks)
    return [values[0]] + [pltpu.roll(values[(-n) % 8], LANE - n, 1) for n in range(1, 8)]


def dot(a, b, ca, cb):
    return lax.dot_general(a, b, (((ca,), (cb,)), ((), ())), preferred_element_type=F32)


def seq_offset(k):
    return (k * 11) % SEQ


def seq_moved(seq, off, sign):
    y, xh, z = seq // 8, (seq // 4) % 2, seq % 4
    dy, dx, dz = off // 8, (off // 4) % 2, off % 4
    return ((y + sign * dy + 4) % 4) * 8 + ((xh + dx) % 2) * 4 + (z + sign * dz + 4) % 4


def exchange_copy(k, src, dst, send, recv):
    me = lax.axis_index("seq")
    peer = seq_moved(me, seq_offset(k), 1)
    return remote(
        src.at[:, pl.ds(aligned(peer * 16, 16), 16), :],
        dst.at[:, pl.ds(aligned(me * 16, 16), 16), :],
        send.at[k],
        recv.at[k],
        (peer, lax.axis_index("chan")),
    )


def exchange_start(src, dst, send, recv, local):
    me = lax.axis_index("seq")
    rows = pl.ds(aligned(me * 16, 16), 16)

    def step(k, _):
        exchange_copy(k, src, dst, send, recv).start()
        return _

    lax.fori_loop(1, SEQ, step, 0)
    copy = pltpu.make_async_copy(src.at[:, rows, :], dst.at[:, rows, :], local)
    copy.start()
    return copy


def exchange_recv(src, dst, send, recv, own):
    own.wait()

    def step(k, _):
        exchange_copy(k, src, dst, send, recv).wait_recv()
        return _

    lax.fori_loop(1, SEQ, step, 0)


def exchange_sent(src, dst, send, recv):
    def step(k, _):
        exchange_copy(k, src, dst, send, recv).wait_send()
        return _

    lax.fori_loop(1, SEQ, step, 0)


def blocks(body):
    def step(i, _):
        row = aligned(i * 16, 16)
        for j in range(3):
            body(i, row, slice(j * LANE, (j + 1) * LANE))
        return _

    lax.fori_loop(0, 32, step, 0)


def main_kernel(
    in_ref, gate_ref, ker_ref, cot_ref, right_ref, left_ref,
    out_ref, gin_ref, ggate_ref, gker_ref, gleft_ref, gright_ref,
    xin, xgate, xker, cot, gated, bsend, brecv, tsend, trecv, tgrp, right, left, work, piece, stage,
    load, own, sems, stores, stage_sems,
):
    me = lax.axis_index("seq")
    chan = lax.axis_index("chan")
    barrier = pltpu.get_barrier_semaphore()

    def hello(k, _):
        pl.semaphore_signal(barrier, inc=1, device_id=(seq_moved(me, seq_offset(k), 1), chan), device_id_type=MESH)
        return _

    loads = {
        "cot0": pltpu.make_async_copy(cot_ref.at[pl.ds(0, 8)], cot.at[:, pl.ds(0, 256), :], load.at[0]),
        "cot1": pltpu.make_async_copy(cot_ref.at[pl.ds(8, 8)], cot.at[:, pl.ds(256, 256), :], load.at[1]),
        "left": pltpu.make_async_copy(left_ref, left, load.at[2]),
        "in": pltpu.make_async_copy(in_ref, xin, load.at[3]),
        "gate": pltpu.make_async_copy(gate_ref, xgate, load.at[4]),
        "right": pltpu.make_async_copy(right_ref, right, load.at[5]),
        "ker": pltpu.make_async_copy(ker_ref, xker, load.at[6]),
    }
    for copy in loads.values():
        copy.start()
    lax.fori_loop(1, SEQ, hello, 0)
    pl.semaphore_wait(barrier, SEQ - 1)
    masks = masks_of(16)

    loads["cot0"].wait()
    loads["cot1"].wait()

    def cot_groups(i, row, lanes):
        values = [cot[n, pl.ds(row, 16), lanes].astype(F32) for n in range(8)]
        for h, value in enumerate(to_groups(values, masks)):
            cot[h, pl.ds(row, 16), lanes] = value.astype(BF)

    blocks(cot_groups)
    loads["left"].wait()

    def back_dot(h, _):
        for half in range(2):
            rows = slice(half * 256, half * 256 + 256)
            work[h, rows, :] = dot(left[h], cot[h, rows, :], 0, 0)
        return _

    lax.fori_loop(0, H, back_dot, 0)

    def back_rows(i, _):
        for j in range(3):
            lanes = slice(j * LANE, (j + 1) * LANE)
            for half in range(2):
                row = aligned(half * 256 + i * 16, 16)
                values = from_groups([work[h, pl.ds(row, 16), lanes] for h in range(8)], masks)
                for n, value in enumerate(values):
                    piece[j, pl.ds(half * 8 + n, 16, stride=16), :] = value
            for k in range(16):
                to = aligned((2 * i + k // 8) * 16, 16)
                bsend[k % 8, pl.ds(to, 16), lanes] = piece[j, k * 16 : k * 16 + 16, :].astype(BF)
        return _

    lax.fori_loop(0, 16, back_rows, 0)
    back = (bsend, brecv, sems.at[0], sems.at[1])
    back_own = exchange_start(*back, own.at[0])

    loads["in"].wait()
    loads["gate"].wait()

    def gate_groups(i, row, lanes):
        rows = pl.ds(row, 16)
        values = [xin[n, rows, lanes].astype(F32) * xgate[n, rows, lanes].astype(F32) for n in range(8)]
        for h, value in enumerate(to_groups(values, masks)):
            gated[h, rows, lanes] = value.astype(BF)

    blocks(gate_groups)
    loads["right"].wait()

    def inner_dot(h, _):
        work[h] = dot(right[h], gated[h], 1, 0)
        return _

    lax.fori_loop(0, H, inner_dot, 0)
    loads["ker"].wait()

    def twist(i, row, lanes):
        rows = pl.ds(row, 16)
        values = from_groups([work[h, rows, lanes] for h in range(8)], masks)
        for n, value in enumerate(values):
            work[n, rows, lanes] = value
            tsend[n, rows, lanes] = (xker[n, rows, lanes].astype(F32) * value).astype(BF)

    blocks(twist)
    exchange_recv(*back, back_own)
    twisted = (tsend, trecv, sems.at[2], sems.at[3])
    twisted_own = exchange_start(*twisted, own.at[1])

    def push(i, row, lanes):
        rows = pl.ds(row, 16)
        values = []
        for n in range(8):
            value = brecv[n, rows, lanes].astype(F32)
            weight = xker[n, rows, lanes].astype(F32)
            xker[n, rows, lanes] = (value * work[n, rows, lanes]).astype(BF)
            values.append(weight * value)
        for h, value in enumerate(to_groups(values, masks)):
            brecv[h, rows, lanes] = value.astype(BF)

    blocks(push)
    save = [pltpu.make_async_copy(xker, gker_ref, stores.at[0])]
    save[0].start()

    def gated_dot(h, _):
        work[h] = dot(right[h], brecv[h], 0, 0)
        return _

    lax.fori_loop(0, H, gated_dot, 0)

    def gate_grads(i, row, lanes):
        rows = pl.ds(row, 16)
        values = from_groups([work[h, rows, lanes] for h in range(8)], masks)
        for n, value in enumerate(values):
            first = xin[n, rows, lanes].astype(F32)
            second = xgate[n, rows, lanes].astype(F32)
            xin[n, rows, lanes] = (value * second).astype(BF)
            xgate[n, rows, lanes] = (value * first).astype(BF)

    blocks(gate_grads)
    save.append(pltpu.make_async_copy(xin, gin_ref, stores.at[1]))
    save.append(pltpu.make_async_copy(xgate, ggate_ref, stores.at[2]))
    save[1].start()
    save[2].start()

    for h in range(H):
        copy = pltpu.make_async_copy(stage.at[h % 2], gright_ref.at[h], stage_sems.at[h % 2])
        if h >= 2:
            copy.wait()
        stage[h % 2] = dot(brecv[h], gated[h], 1, 1)
        copy.start()
    for slot in range(2):
        pltpu.make_async_copy(stage.at[slot], gright_ref.at[slot], stage_sems.at[slot]).wait()

    exchange_recv(*twisted, twisted_own)

    def twist_groups(i, _):
        for j in range(3):
            lanes = slice(j * LANE, (j + 1) * LANE)
            for k in range(16):
                at = aligned((2 * i + k // 8) * 16, 16)
                piece[j, k * 16 : k * 16 + 16, :] = trecv[k % 8, pl.ds(at, 16), lanes].astype(F32)
            for half in range(2):
                values = [piece[j, pl.ds(half * 8 + n, 16, stride=16), :] for n in range(8)]
                for h, value in enumerate(to_groups(values, masks)):
                    tgrp[h, pl.ds(aligned(half * 256 + i * 16, 16), 16), lanes] = value.astype(BF)
        return _

    lax.fori_loop(0, 16, twist_groups, 0)

    def outer_dot(h, _):
        for half in range(2):
            rows = slice(half * 256, half * 256 + 256)
            work[h, rows, :] = dot(left[h], tgrp[h, rows, :], 1, 0)
        return _

    lax.fori_loop(0, H, outer_dot, 0)

    def out_rows(i, row, lanes):
        rows = pl.ds(row, 16)
        values = from_groups([work[h, rows, lanes] for h in range(8)], masks)
        for n, value in enumerate(values):
            trecv[n, rows, lanes] = value.astype(BF)

    blocks(out_rows)
    save.append(pltpu.make_async_copy(trecv.at[:, pl.ds(0, 256), :], out_ref.at[pl.ds(0, 8)], stores.at[3]))
    save.append(pltpu.make_async_copy(trecv.at[:, pl.ds(256, 256), :], out_ref.at[pl.ds(8, 8)], stores.at[4]))
    save[3].start()
    save[4].start()
    for h in range(H):
        value = dot(cot[h, :256, :], tgrp[h, :256, :], 1, 1) + dot(cot[h, 256:, :], tgrp[h, 256:, :], 1, 1)
        copy = pltpu.make_async_copy(stage.at[h % 2, pl.ds(0, 256), pl.ds(0, 256)], gleft_ref.at[h], stage_sems.at[h % 2])
        if h >= 2:
            copy.wait()
        stage[h % 2, :256, :256] = value
        copy.start()
    for slot in range(2):
        pltpu.make_async_copy(stage.at[slot, pl.ds(0, 256), pl.ds(0, 256)], gleft_ref.at[slot], stage_sems.at[slot]).wait()
    exchange_sent(*back)
    exchange_sent(*twisted)
    for copy in save:
        copy.wait()


def mix(inputs, gate_values, kernel, grad_out, right, left):
    hbm = pl.BlockSpec(memory_space=pl.ANY)
    rows = pltpu.VMEM((8, B, 384), BF)
    return pl.pallas_call(
        main_kernel,
        out_shape=(
            jax.ShapeDtypeStruct((16, A, 384), BF),
            jax.ShapeDtypeStruct((8, B, 384), BF),
            jax.ShapeDtypeStruct((8, B, 384), BF),
            jax.ShapeDtypeStruct((8, B, 384), BF),
            jax.ShapeDtypeStruct((H, A, A), F32),
            jax.ShapeDtypeStruct((H, B, B), F32),
        ),
        in_specs=[hbm] * 6,
        out_specs=(hbm,) * 6,
        scratch_shapes=[rows] * 10
        + [
            pltpu.VMEM((H, B, B), BF),
            pltpu.VMEM((H, A, A), BF),
            pltpu.VMEM((8, B, 384), F32),
            pltpu.VMEM((3, 256, LANE), F32),
            pltpu.VMEM((2, B, B), F32),
            pltpu.SemaphoreType.DMA((7,)),
            pltpu.SemaphoreType.DMA((2,)),
            pltpu.SemaphoreType.DMA((4, SEQ)),
            pltpu.SemaphoreType.DMA((5,)),
            pltpu.SemaphoreType.DMA((2,)),
        ],
        compiler_params=pltpu.CompilerParams(collective_id=1, has_side_effects=True, vmem_limit_bytes=60 << 20),
        name="mix",
    )(inputs, gate_values, kernel, grad_out, right, left)


def reduce_kernel(
    gright_ref, gleft_ref, right_out, left_out,
    own_r, own_l, sib_r, sib_l, got_r, got_l, d0_r, d1_r, d2_r, d0_l, d1_l, d2_l, full_r, full_l, piece,
    core_sems, axis_sems,
):
    xyz, core = place()
    sibling = device_at(xyz, 1 - core)
    greet(chip_friends(xyz, core))
    half_r = pl.ds(aligned(core * 256, 256), 256)
    half_l = pl.ds(aligned(core * 128, 128), 128)
    other_r = pl.ds(aligned((1 - core) * 256, 256), 256)
    other_l = pl.ds(aligned((1 - core) * 128, 128), 128)

    def left_piece(seq, lanes):
        for h in range(H):
            value = gleft_ref[h, pl.ds(aligned(seq * 8, 8), 8), lanes]
            piece[h * 4 : h * 4 + 4, :] = value[:4]
            piece[32 + h * 4 : 32 + h * 4 + 4, :] = value[4:]

    def pack_left(seq, _):
        cy, cx, cz = seq // 8, (seq // 4) % 2, seq % 4
        left_piece(seq, other_l)
        for lo in range(2):
            sib_l[cx * 2 + lo, cy, cz] = piece[lo * 32 : lo * 32 + 32, :].astype(BF)
        return _

    def right_tile(seq, lo, g, lanes):
        rows = pl.ds(aligned(seq * 16 + lo * 8, 8), 8)
        return jnp.concatenate([gright_ref[2 * g, rows, lanes], gright_ref[2 * g + 1, rows, lanes]], axis=0)

    def pack_right(seq, _):
        cy, cx, cz = seq // 8, (seq // 4) % 2, seq % 4
        for lo in range(2):
            for g in range(4):
                sib_r[cx * 2 + lo, cy, cz, g * 16 : g * 16 + 16, :] = right_tile(seq, lo, g, other_r).astype(BF)
        return _

    lax.fori_loop(0, SEQ, pack_left, 0)
    first_l = remote(sib_l, got_l, core_sems.at[0, 0], core_sems.at[1, 0], sibling)
    first_l.start()
    lax.fori_loop(0, SEQ, pack_right, 0)
    first_r = remote(sib_r, got_r, core_sems.at[0, 1], core_sems.at[1, 1], sibling)
    first_r.start()

    def sum_left(seq, _):
        cy, cx, cz = seq // 8, (seq // 4) % 2, seq % 4
        left_piece(seq, half_l)
        for lo in range(2):
            value = piece[lo * 32 : lo * 32 + 32, :] + got_l[cx * 2 + lo, cy, cz].astype(F32)
            own_l[cx * 2 + lo, cy, cz] = value.astype(BF)
        return _

    def sum_right(seq, _):
        cy, cx, cz = seq // 8, (seq // 4) % 2, seq % 4
        for lo in range(2):
            for g in range(4):
                rows = slice(g * 16, g * 16 + 16)
                value = right_tile(seq, lo, g, half_r) + got_r[cx * 2 + lo, cy, cz, rows, :].astype(F32)
                own_r[cx * 2 + lo, cy, cz, rows, :] = value.astype(BF)
        return _

    first_l.wait()
    lax.fori_loop(0, SEQ, sum_left, 0)
    first_r.wait()
    lax.fori_loop(0, SEQ, sum_right, 0)

    parts = [(own_l, (d0_l, d1_l, d2_l), full_l, core) + part for part in LEFT_PARTS] + [
        (own_r, (d0_r, d1_r, d2_r), full_r, core * 2) + part for part in RIGHT_PARTS
    ]
    stages = {}

    def add(number, stage):
        buf, heaps, full, first_lane, row, rows, order = parts[number]
        rest = order[stage + 1 :]
        span = pl.ds(row, rows)

        def one(i, _):
            at = {order[n]: xyz[order[n]] for n in range(stage + 1)}
            spots = []
            left_over = i
            for axis in reversed(sorted(rest)):
                at[axis] = left_over % 4
                spots.insert(0, left_over % 4)
                left_over = left_over // 4
            index = (at[0], at[1], at[2], span)
            value = buf[index].astype(F32)
            for step in range(3):
                value = value + heaps[stage][(step, *spots, span)].astype(F32)
            if stage == 2:
                for n in range(value.shape[1] // LANE):
                    full[first_lane + n, span, :] = value[:, n * LANE : (n + 1) * LANE]
            else:
                buf[index] = value.astype(BF)
            return _

        if rest:
            lax.fori_loop(0, 4 ** len(rest), one, 0)
        else:
            one(0, 0)

    for stage in range(4):
        for number, (buf, heaps, _, _, row, rows, order) in enumerate(parts):
            if stage > 0:
                for copy in stages[number]:
                    copy.wait()
                add(number, stage - 1)
            if stage == 3:
                continue
            span = pl.ds(row, rows)
            stages[number] = []
            for step in (1, 2, 3):
                to = moved(xyz, order[stage], step)
                index = tuple(slice(None) if axis in order[stage + 1 :] else to[axis] for axis in range(3))
                heap = heaps[stage].at[(step - 1,) + (slice(None),) * (2 - stage) + (span,)]
                stages[number].append(
                    remote(
                        buf.at[index + (span,)],
                        heap,
                        axis_sems.at[0, number, stage, step - 1],
                        axis_sems.at[1, number, stage, step - 1],
                        device_at(to, core),
                    )
                )
            for copy in stages[number]:
                copy.start()
    last = [
        remote(full_l.at[core], full_l.at[core], core_sems.at[0, 2], core_sems.at[1, 2], sibling),
        remote(full_r.at[pl.ds(core * 2, 2)], full_r.at[pl.ds(core * 2, 2)], core_sems.at[0, 3], core_sems.at[1, 3], sibling),
    ]
    for copy in last:
        copy.start()
    for copy in last:
        copy.wait()
    for lane in range(4):
        lanes = slice(lane * LANE, (lane + 1) * LANE)
        for r in range(4):
            right_out[r, :, lanes] = full_r[lane, pl.ds(core * 4 + r, 8, stride=8), :] / math.sqrt(A * C / H)
        if lane < 2:
            for r in range(2):
                left_out[r, :, lanes] = full_l[lane, pl.ds(core * 2 + r, 8, stride=4), :] / math.sqrt(B * C / H)


def reduce_tiles(gright, gleft):
    vmem = pl.BlockSpec(memory_space=pltpu.VMEM)
    return pl.pallas_call(
        reduce_kernel,
        out_shape=(jax.ShapeDtypeStruct((4, H, B), F32), jax.ShapeDtypeStruct((2, H, A), F32)),
        in_specs=[vmem, vmem],
        out_specs=(vmem, vmem),
        scratch_shapes=[
            pltpu.VMEM((4, 4, 4, 64, 256), BF),
            pltpu.VMEM((4, 4, 4, 32, 128), BF),
            pltpu.VMEM((4, 4, 4, 64, 256), BF),
            pltpu.VMEM((4, 4, 4, 32, 128), BF),
            pltpu.VMEM((4, 4, 4, 64, 256), BF),
            pltpu.VMEM((4, 4, 4, 32, 128), BF),
            pltpu.VMEM((3, 4, 4, 64, 256), BF),
            pltpu.VMEM((3, 4, 64, 256), BF),
            pltpu.VMEM((3, 64, 256), BF),
            pltpu.VMEM((3, 4, 4, 32, 128), BF),
            pltpu.VMEM((3, 4, 32, 128), BF),
            pltpu.VMEM((3, 32, 128), BF),
            pltpu.VMEM((4, 64, LANE), F32),
            pltpu.VMEM((2, 32, LANE), F32),
            pltpu.VMEM((64, LANE), F32),
            pltpu.SemaphoreType.DMA((2, 4)),
            pltpu.SemaphoreType.DMA((2, 4, 3, 3)),
        ],
        compiler_params=pltpu.CompilerParams(collective_id=2, has_side_effects=True, vmem_limit_bytes=48 << 20),
        name="reduce_tiles",
    )(gright, gleft)


def on_device(inputs, gate_values, kernel, grad_out, left_tiles, right_tiles):
    right, left = gather_tiles(right_tiles.reshape(32, B), left_tiles.reshape(16, A))
    output, grad_inputs, grad_gates, grad_kernel, gleft, gright = mix(
        inputs, gate_values, kernel, grad_out, right, left
    )
    grad_right, grad_left = reduce_tiles(gright, gleft)
    return (output, grad_inputs, grad_gates, grad_kernel, grad_left, grad_right)


def solution(mesh):
    specs = (P("seq", None, "chan"),) * 4 + (P(("seq", "chan"), None, None),) * 2
    return jax.shard_map(on_device, mesh=mesh, in_specs=specs, out_specs=specs, check_vma=False)
```

```python
import functools
import math

import jax
import jax.numpy as jnp
from jax import lax
from jax.experimental import pallas as pl
from jax.experimental.pallas import tpu as pltpu
from jax.sharding import PartitionSpec as P

MESH = pl.DeviceIdType.MESH
BF = jnp.bfloat16
F32 = jnp.float32
A = 256
B = 512
C = 1536
H = 8
LANE = 128
SEQ = 32
RIGHT_PARTS = ((0, 256, (0, 1, 2)), (256, 128, (1, 2, 0)), (384, 128, (2, 0, 1)))
LEFT_PARTS = ((0, 128, (1, 2, 0)), (128, 128, (2, 0, 1)))


def place():
    seq = lax.axis_index("seq")
    chan = lax.axis_index("chan")
    x = ((seq // 4) % 2) * 2 + chan // 2
    return (x, seq // 8, seq % 4), chan % 2


def device_at(xyz, core):
    x, y, z = xyz
    return (y * 8 + (x // 2) * 4 + z, (x % 2) * 2 + core)


def moved(xyz, axis, step):
    new = list(xyz)
    new[axis] = (xyz[axis] + step) % 4
    return tuple(new)


def chip_friends(xyz, core):
    return [device_at(xyz, 1 - core)] + [
        device_at(moved(xyz, axis, step), core) for axis in range(3) for step in (1, 2, 3)
    ]


def remote(src, dst, send, recv, device):
    return pltpu.make_async_remote_copy(
        src_ref=src, dst_ref=dst, send_sem=send, recv_sem=recv, device_id=device, device_id_type=MESH
    )


def aligned(value, multiple):
    return pl.multiple_of(value, multiple)


def masks_of(rows):
    lane = lax.broadcasted_iota(jnp.int32, (rows, LANE), 1)
    return [(lane & bit) != 0 for bit in (1, 2, 4)]


def turn(values, masks):
    for bit, mask in zip((1, 2, 4), masks):
        values = [jnp.where(mask, values[(i + bit) % 8], values[i]) for i in range(8)]
    return values


def to_groups(values, masks):
    values = turn([v if n == 0 else pltpu.roll(v, n, 1) for n, v in enumerate(values)], masks)
    return [values[(-h) % 8] for h in range(8)]


def from_groups(values, masks):
    values = turn(values, masks)
    return [values[0]] + [pltpu.roll(values[(-n) % 8], LANE - n, 1) for n in range(1, 8)]


def dot(a, b, ca, cb):
    return lax.dot_general(a, b, (((ca,), (cb,)), ((), ())), preferred_element_type=F32)


def seq_offset(k):
    return (k * 11) % SEQ


def seq_moved(seq, off):
    y, xh, z = seq // 8, (seq // 4) % 2, seq % 4
    dy, dx, dz = off // 8, (off // 4) % 2, off % 4
    return ((y + dy) % 4) * 8 + ((xh + dx) % 2) * 4 + (z + dz) % 4


class Exchange:
    def __init__(self, src, dst, send, recv, local):
        self.src, self.dst, self.send, self.recv, self.local = src, dst, send, recv, local

    def copy(self, j, k):
        me = lax.axis_index("seq")
        peer = seq_moved(me, seq_offset(k))
        lanes = pl.ds(j * LANE, LANE)
        return remote(
            self.src.at[:, pl.ds(aligned(peer * 16, 16), 16), lanes],
            self.dst.at[:, pl.ds(aligned(me * 16, 16), 16), lanes],
            self.send.at[j, k],
            self.recv.at[j, k],
            (peer, lax.axis_index("chan")),
        )

    def own(self, j):
        rows = pl.ds(aligned(lax.axis_index("seq") * 16, 16), 16)
        lanes = pl.ds(j * LANE, LANE)
        return pltpu.make_async_copy(self.src.at[:, rows, lanes], self.dst.at[:, rows, lanes], self.local.at[j])

    def start(self, j):
        def step(k, _):
            self.copy(j, k).start()
            return _

        lax.fori_loop(1, SEQ, step, 0)
        self.own(j).start()

    def arrived(self, j):
        def step(k, _):
            self.copy(j, k).wait_recv()
            return _

        self.own(j).wait()
        lax.fori_loop(1, SEQ, step, 0)

    def sent(self, j):
        def step(k, _):
            self.copy(j, k).wait_send()
            return _

        lax.fori_loop(1, SEQ, step, 0)


class Gather:
    def __init__(self, buf, rows, lane, lanes, order, send, recv):
        self.buf, self.rows, self.lanes, self.order = buf, rows, pl.ds(lane, lanes), order
        self.send, self.recv = send, recv

    def copies(self, stage):
        xyz, core = place()
        index = tuple(slice(None) if axis in self.order[:stage] else xyz[axis] for axis in range(3))
        ref = self.buf.at[index + (pl.ds(aligned(core * self.rows, self.rows), self.rows), self.lanes)]
        return [
            remote(
                ref,
                ref,
                self.send.at[stage, step - 1],
                self.recv.at[stage, step - 1],
                device_at(moved(xyz, self.order[stage], step), core),
            )
            for step in (1, 2, 3)
        ]

    def start(self, stage):
        for copy in self.copies(stage):
            copy.start()

    def wait(self, stage):
        for copy in self.copies(stage):
            copy.wait()


class Reduce:
    def __init__(self, buf, heaps, out, scale, lane, lanes, order, send, recv):
        self.buf, self.heaps, self.out, self.scale = buf, heaps, out, scale
        self.lanes, self.order, self.send, self.recv = pl.ds(lane, lanes), order, send, recv

    def copies(self, stage):
        xyz, core = place()
        axis = self.order[stage]
        found = []
        for step in (1, 2, 3):
            to = moved(xyz, axis, step)
            index = tuple(slice(None) if n in self.order[stage + 1 :] else to[n] for n in range(3))
            found.append(
                remote(
                    self.buf.at[index + (slice(None), self.lanes)],
                    self.heaps[stage].at[(step - 1,) + (slice(None),) * (3 - stage) + (self.lanes,)],
                    self.send.at[stage, step - 1],
                    self.recv.at[stage, step - 1],
                    device_at(to, core),
                )
            )
        return found

    def start(self, stage):
        for copy in self.copies(stage):
            copy.start()

    def finish(self, stage):
        for copy in self.copies(stage):
            copy.wait()
        xyz, _ = place()
        rest = sorted(self.order[stage + 1 :])

        def one(i, carry):
            at = list(xyz)
            spots = [i // 4, i % 4][2 - len(rest) :]
            for axis, spot in zip(rest, spots):
                at[axis] = spot
            index = (*at, slice(None), self.lanes)
            value = self.buf[index].astype(F32)
            for step in range(3):
                value = value + self.heaps[stage][(step, *spots, slice(None), self.lanes)].astype(F32)
            if stage == 2:
                self.out[:, self.lanes] = value / self.scale
            else:
                self.buf[index] = value.astype(BF)
            return carry

        if rest:
            lax.fori_loop(0, 4 ** len(rest), one, 0)
        else:
            one(0, 0)


def blocks(body, j):
    def step(i, _):
        body(i, aligned(i * 16, 16), slice(j * LANE, (j + 1) * LANE))
        return _

    lax.fori_loop(0, 32, step, 0)


def chip_of(seq):
    return ((seq // 4) % 2) * 2, seq // 8, seq % 4


def layer_kernel(
    in_ref, gate_ref, ker_ref, cot_ref, right_ref, left_ref,
    out_ref, gin_ref, ggate_ref, gker_ref, gleft_ref, gright_ref,
    xin, xgate, xker, cot, gated, bsend, brecv, tsend, trecv, right, left, work, gsum, piece, raw_r, raw_l,
    own_r, sib_r, got_r, d0_r, d1_r, d2_r, own_l, sib_l, got_l, d0_l, d1_l, d2_l,
    load, own, sems, stores, core_sems, gather_sems, reduce_sems,
):
    me = lax.axis_index("seq")
    chan = lax.axis_index("chan")
    xyz, core = place()
    sibling = device_at(xyz, 1 - core)
    barrier = pltpu.get_barrier_semaphore()
    tgrp = bsend

    loads = {
        "cot0": pltpu.make_async_copy(cot_ref.at[pl.ds(0, 8)], cot.at[:, pl.ds(0, 256), :], load.at[0]),
        "cot1": pltpu.make_async_copy(cot_ref.at[pl.ds(8, 8)], cot.at[:, pl.ds(256, 256), :], load.at[1]),
        "in": pltpu.make_async_copy(in_ref, xin, load.at[2]),
        "gate": pltpu.make_async_copy(gate_ref, xgate, load.at[3]),
        "ker": pltpu.make_async_copy(ker_ref, xker, load.at[4]),
        "left": pltpu.make_async_copy(
            left_ref, raw_l.at[(*xyz, pl.ds(aligned(core * 16, 16), 16))], load.at[5]
        ),
        "right": pltpu.make_async_copy(
            right_ref, raw_r.at[(*xyz, pl.ds(aligned(core * 32, 32), 32))], load.at[6]
        ),
    }

    def hello(k, _):
        pl.semaphore_signal(barrier, inc=1, device_id=(seq_moved(me, seq_offset(k)), chan), device_id_type=MESH)
        return _

    lax.fori_loop(1, SEQ, hello, 0)
    friends = chip_friends(xyz, core)
    for device in friends:
        pl.semaphore_signal(barrier, inc=1, device_id=device, device_id_type=MESH)
    for name in ("left", "right", "cot0", "cot1", "in", "gate", "ker"):
        loads[name].start()
    pl.semaphore_wait(barrier, SEQ - 1 + len(friends))
    loads["left"].wait()
    loads["right"].wait()
    masks = masks_of(16)

    gather_l = [
        Gather(raw_l, 16, *part, gather_sems.at[0, n], gather_sems.at[1, n]) for n, part in enumerate(LEFT_PARTS)
    ]
    gather_r = [
        Gather(raw_r, 32, *part, gather_sems.at[0, 2 + n], gather_sems.at[1, 2 + n])
        for n, part in enumerate(RIGHT_PARTS)
    ]
    mine_l = raw_l.at[:, :, :, pl.ds(aligned(core * 16, 16), 16), :]
    mine_r = raw_r.at[:, :, :, pl.ds(aligned(core * 32, 32), 32), :]
    swap_l = remote(mine_l, mine_l, core_sems.at[0, 0], core_sems.at[1, 0], sibling)
    swap_r = remote(mine_r, mine_r, core_sems.at[0, 1], core_sems.at[1, 1], sibling)
    back = Exchange(bsend, brecv, sems.at[0], sems.at[1], own.at[0])
    twisted = Exchange(tsend, trecv, sems.at[2], sems.at[3], own.at[1])

    def cot_groups(i, row, lanes):
        values = [cot[n, pl.ds(row, 16), lanes].astype(F32) for n in range(8)]
        for h, value in enumerate(to_groups(values, masks)):
            cot[h, pl.ds(row, 16), lanes] = value.astype(BF)

    for part in gather_l + gather_r:
        part.start(0)
    loads["cot0"].wait()
    loads["cot1"].wait()
    blocks(cot_groups, 0)
    for stage in range(2):
        for part in gather_l:
            part.wait(stage)
            part.start(stage + 1)
        if stage == 0:
            for part in gather_r:
                part.wait(0)
                part.start(1)
        blocks(cot_groups, stage + 1)
    for part in gather_l:
        part.wait(2)
    swap_l.start()
    for part in gather_r:
        part.wait(1)
        part.start(2)
    swap_l.wait()

    def left_rows(pair, _):
        cx, cy, cz = chip_of(pair * 2)
        for lane in range(2):
            lanes = slice(lane * LANE, (lane + 1) * LANE)
            for n in range(4):
                piece[lane, n * 32 : n * 32 + 32, :] = raw_l[cx + n % 2, cy, cz + n // 2, :, lanes].astype(F32)
            for h in range(H):
                left[h, pl.ds(aligned(pair * 16, 16), 16), lanes] = piece[lane, pl.ds(h, 16, stride=8), :].astype(BF)
        return _

    lax.fori_loop(0, 16, left_rows, 0)

    def both(ref, h, lanes):
        return jnp.concatenate([ref[h, :256, lanes], ref[h, 256:, lanes]], axis=1)

    def back_rows(j):
        lanes = slice(j * LANE, (j + 1) * LANE)

        def product(h, _):
            value = dot(left[h], both(cot, h, lanes), 0, 0)
            work[j, pl.ds(aligned(h * 512, 512), 256), :] = value[:, :LANE]
            work[j, pl.ds(aligned(h * 512 + 256, 256), 256), :] = value[:, LANE:]
            return _

        lax.fori_loop(0, H, product, 0)

        def rows(i, _):
            for half in range(2):
                values = [work[j, pl.ds(aligned(h * 512 + half * 256 + i * 16, 16), 16), :] for h in range(8)]
                for n, value in enumerate(from_groups(values, masks)):
                    piece[j, pl.ds(half * 8 + n, 16, stride=16), :] = value
            for k in range(16):
                to = aligned((2 * i + k // 8) * 16, 16)
                bsend[k % 8, pl.ds(to, 16), lanes] = piece[j, k * 16 : k * 16 + 16, :].astype(BF)
            return _

        lax.fori_loop(0, 16, rows, 0)

    for j in range(3):
        back_rows(j)
        back.start(j)

    loads["in"].wait()
    loads["gate"].wait()

    def gate_groups(i, row, lanes):
        rows = pl.ds(row, 16)
        values = [xin[n, rows, lanes].astype(F32) * xgate[n, rows, lanes].astype(F32) for n in range(8)]
        for h, value in enumerate(to_groups(values, masks)):
            gated[h, rows, lanes] = value.astype(BF)

    for j in range(3):
        blocks(gate_groups, j)
    for part in gather_r:
        part.wait(2)
    swap_r.start()
    loads["ker"].wait()
    swap_r.wait()

    def right_rows(seq, _):
        cx, cy, cz = chip_of(seq)
        for lane in range(4):
            lanes = slice(lane * LANE, (lane + 1) * LANE)
            for lo in range(2):
                piece[lane, lo * 64 : lo * 64 + 64, :] = raw_r[cx + lo, cy, cz, :, lanes].astype(F32)
            for h in range(H):
                right[h, pl.ds(aligned(seq * 16, 16), 16), lanes] = piece[lane, pl.ds(h, 16, stride=8), :].astype(BF)
        return _

    lax.fori_loop(0, 32, right_rows, 0)

    def spread(h, value):
        for j in range(3):
            work[j, pl.ds(aligned(h * 512, 512), 512), :] = value[:, j * LANE : (j + 1) * LANE]

    def inner_dot(h, _):
        spread(h, dot(right[h], gated[h], 1, 0))
        return _

    lax.fori_loop(0, H, inner_dot, 0)

    def group_rows(j, row):
        return [work[j, pl.ds(aligned(h * 512 + row, 16), 16), :] for h in range(8)]

    def twist(j):
        def body(i, row, lanes):
            rows = pl.ds(row, 16)
            for n, value in enumerate(from_groups(group_rows(j, row), masks)):
                work[j, pl.ds(aligned(n * 512 + row, 16), 16), :] = value
                tsend[n, rows, lanes] = (xker[n, rows, lanes].astype(F32) * value).astype(BF)

        blocks(body, j)

    def push(j):
        def body(i, row, lanes):
            rows = pl.ds(row, 16)
            values = []
            spectral = group_rows(j, row)
            for n in range(8):
                value = brecv[n, rows, lanes].astype(F32)
                weight = xker[n, rows, lanes].astype(F32)
                xker[n, rows, lanes] = (value * spectral[n]).astype(BF)
                values.append(weight * value)
            for h, value in enumerate(to_groups(values, masks)):
                brecv[h, rows, lanes] = value.astype(BF)

        blocks(body, j)

    for j in range(3):
        twist(j)
    for j in range(3):
        back.arrived(j)
        twisted.start(j)
        push(j)
    save = [pltpu.make_async_copy(xker, gker_ref, stores.at[0])]
    save[0].start()

    def pack_right(block):
        def product(h, _):
            value = dot(brecv[h, block * 128 : block * 128 + 128, :], gated[h], 1, 1)
            for lane in range(4):
                row = aligned(h * 512 + lane * 128, 128)
                work[0, pl.ds(row, 128), :] = value[:, lane * LANE : (lane + 1) * LANE]
            return _

        lax.fori_loop(0, H, product, 0)

        def rows(n, _):
            cx, cy, cz = chip_of(block * 8 + n)
            for lane in range(4):
                lanes = slice(lane * LANE, (lane + 1) * LANE)
                for lo in range(2):
                    for buf, which in ((sib_r, 1 - core), (own_r, core)):
                        row = lane * 128 + n * 16 + lo * 8 + which * 4
                        for half in range(2):
                            tile = jnp.concatenate(
                                [work[0, pl.ds(row + half * 2 + r, 8, stride=512), :] for r in range(2)], axis=0
                            )
                            buf[cx + lo, cy, cz, half * 16 : half * 16 + 16, lanes] = tile.astype(BF)
            return _

        lax.fori_loop(0, 8, rows, 0)

    for block in range(4):
        pack_right(block)
    pair_r = remote(sib_r, got_r, core_sems.at[0, 2], core_sems.at[1, 2], sibling)
    pair_r.start()
    reduce_r = [
        Reduce(own_r, (d0_r, d1_r, d2_r), gright_ref, math.sqrt(A * C / H), *part, reduce_sems.at[0, 2 + n], reduce_sems.at[1, 2 + n])
        for n, part in enumerate(RIGHT_PARTS)
    ]
    reduce_l = [
        Reduce(own_l, (d0_l, d1_l, d2_l), gleft_ref, math.sqrt(B * C / H), *part, reduce_sems.at[0, n], reduce_sems.at[1, n])
        for n, part in enumerate(LEFT_PARTS)
    ]

    def gated_dot(h, _):
        spread(h, dot(right[h], brecv[h], 0, 0))
        return _

    lax.fori_loop(0, H, gated_dot, 0)
    pair_r.wait()

    def add_pair(i, _):
        index = (i // 16, (i // 4) % 4, i % 4)
        own_r[index] = (own_r[index].astype(F32) + got_r[index].astype(F32)).astype(BF)
        return _

    lax.fori_loop(0, 64, add_pair, 0)
    for part in reduce_r:
        part.start(0)

    def gate_grads(j):
        def body(i, row, lanes):
            rows = pl.ds(row, 16)
            for n, value in enumerate(from_groups(group_rows(j, row), masks)):
                first = xin[n, rows, lanes].astype(F32)
                second = xgate[n, rows, lanes].astype(F32)
                xin[n, rows, lanes] = (value * second).astype(BF)
                xgate[n, rows, lanes] = (value * first).astype(BF)

        blocks(body, j)

    for j in range(3):
        gate_grads(j)
    save.append(pltpu.make_async_copy(xin, gin_ref, stores.at[1]))
    save.append(pltpu.make_async_copy(xgate, ggate_ref, stores.at[2]))
    save[1].start()
    save[2].start()
    for j in range(3):
        back.sent(j)

    def twist_groups(j):
        lanes = slice(j * LANE, (j + 1) * LANE)

        def rows(i, _):
            for k in range(16):
                at = aligned((2 * i + k // 8) * 16, 16)
                piece[j, k * 16 : k * 16 + 16, :] = trecv[k % 8, pl.ds(at, 16), lanes].astype(F32)
            for half in range(2):
                values = [piece[j, pl.ds(half * 8 + n, 16, stride=16), :] for n in range(8)]
                for h, value in enumerate(to_groups(values, masks)):
                    tgrp[h, pl.ds(aligned(half * 256 + i * 16, 16), 16), lanes] = value.astype(BF)
            return _

        lax.fori_loop(0, 16, rows, 0)

    def left_terms(j):
        lanes = slice(j * LANE, (j + 1) * LANE)

        def product(h, _):
            value = dot(both(cot, h, lanes), both(tgrp, h, lanes), 1, 1)
            rows = pl.ds(aligned(h * 256, 256), 256)
            for lane in range(2):
                term = value[:, lane * LANE : (lane + 1) * LANE]
                gsum[lane, rows, :] = term if j == 0 else gsum[lane, rows, :] + term
            return _

        lax.fori_loop(0, H, product, 0)

    def outer(j):
        lanes = slice(j * LANE, (j + 1) * LANE)

        def product(h, _):
            value = dot(left[h], both(tgrp, h, lanes), 1, 0)
            work[j, pl.ds(aligned(h * 512, 512), 256), :] = value[:, :LANE]
            work[j, pl.ds(aligned(h * 512 + 256, 256), 256), :] = value[:, LANE:]
            return _

        lax.fori_loop(0, H, product, 0)

        def body(i, row, lanes):
            for n, value in enumerate(from_groups(group_rows(j, row), masks)):
                trecv[n, pl.ds(row, 16), lanes] = value.astype(BF)

        blocks(body, j)

    for j in range(3):
        twisted.arrived(j)
        twist_groups(j)
        left_terms(j)
        if j < 2:
            for part in reduce_r:
                part.finish(j)
                part.start(j + 1)
            outer(j)

    def left_tile(seq, lo, which, lane):
        row = seq * 8 + lo * 4 + which * 2
        return jnp.concatenate([gsum[lane, pl.ds(row + r, 8, stride=256), :] for r in range(2)], axis=0)

    def pack_left(seq, _):
        cx, cy, cz = chip_of(seq)
        for lo in range(2):
            for lane in range(2):
                lanes = slice(lane * LANE, (lane + 1) * LANE)
                sib_l[cx + lo, cy, cz, :, lanes] = left_tile(seq, lo, 1 - core, lane).astype(BF)
        return _

    def add_left(seq, _):
        cx, cy, cz = chip_of(seq)
        for lo in range(2):
            for lane in range(2):
                lanes = slice(lane * LANE, (lane + 1) * LANE)
                value = left_tile(seq, lo, core, lane) + got_l[cx + lo, cy, cz, :, lanes].astype(F32)
                own_l[cx + lo, cy, cz, :, lanes] = value.astype(BF)
        return _

    lax.fori_loop(0, SEQ, pack_left, 0)
    pair_l = remote(sib_l, got_l, core_sems.at[0, 3], core_sems.at[1, 3], sibling)
    pair_l.start()
    for part in reduce_r:
        part.finish(2)
    pair_l.wait()
    lax.fori_loop(0, SEQ, add_left, 0)
    for part in reduce_l:
        part.start(0)
    outer(2)
    save.append(pltpu.make_async_copy(trecv.at[:, pl.ds(0, 256), :], out_ref.at[pl.ds(0, 8)], stores.at[3]))
    save.append(pltpu.make_async_copy(trecv.at[:, pl.ds(256, 256), :], out_ref.at[pl.ds(8, 8)], stores.at[4]))
    save[3].start()
    save[4].start()
    for stage in range(3):
        for part in reduce_l:
            part.finish(stage)
            if stage < 2:
                part.start(stage + 1)
    for j in range(3):
        twisted.sent(j)
    for copy in save:
        copy.wait()


def layer(inputs, gate_values, kernel, grad_out, right, left):
    hbm = pl.BlockSpec(memory_space=pl.ANY)
    vmem = pl.BlockSpec(memory_space=pltpu.VMEM)
    rows = pltpu.VMEM((8, B, 384), BF)

    def heap(rows, lanes):
        block = (rows, lanes)
        return [pltpu.VMEM((4, 4, 4) + block, BF)] * 3 + [
            pltpu.VMEM((3, 4, 4) + block, BF),
            pltpu.VMEM((3, 4) + block, BF),
            pltpu.VMEM((3,) + block, BF),
        ]

    return pl.pallas_call(
        layer_kernel,
        out_shape=(
            jax.ShapeDtypeStruct((16, A, 384), BF),
            jax.ShapeDtypeStruct((8, B, 384), BF),
            jax.ShapeDtypeStruct((8, B, 384), BF),
            jax.ShapeDtypeStruct((8, B, 384), BF),
            jax.ShapeDtypeStruct((16, A), F32),
            jax.ShapeDtypeStruct((32, B), F32),
        ),
        in_specs=[hbm] * 6,
        out_specs=(hbm,) * 4 + (vmem,) * 2,
        scratch_shapes=[rows] * 9
        + [
            pltpu.VMEM((H, B, B), BF),
            pltpu.VMEM((H, A, A), BF),
            pltpu.VMEM((3, H * B, LANE), F32),
            pltpu.VMEM((2, H * A, LANE), F32),
            pltpu.VMEM((4, 256, LANE), F32),
            pltpu.VMEM((4, 4, 4, 64, B), BF),
            pltpu.VMEM((4, 4, 4, 32, A), BF),
        ]
        + heap(32, B)
        + heap(16, A)
        + [
            pltpu.SemaphoreType.DMA((7,)),
            pltpu.SemaphoreType.DMA((2, 3)),
            pltpu.SemaphoreType.DMA((4, 3, SEQ)),
            pltpu.SemaphoreType.DMA((5,)),
            pltpu.SemaphoreType.DMA((2, 4)),
            pltpu.SemaphoreType.DMA((2, 5, 3, 3)),
            pltpu.SemaphoreType.DMA((2, 5, 3, 3)),
        ],
        compiler_params=pltpu.CompilerParams(collective_id=0, has_side_effects=True, vmem_limit_bytes=62 << 20),
        name="layer",
    )(inputs, gate_values, kernel, grad_out, right, left)


def on_device(inputs, gate_values, kernel, grad_out, left_tiles, right_tiles):
    output, grad_inputs, grad_gates, grad_kernel, grad_left, grad_right = layer(
        inputs, gate_values, kernel, grad_out, right_tiles.reshape(32, B), left_tiles.reshape(16, A)
    )
    return (
        output,
        grad_inputs,
        grad_gates,
        grad_kernel,
        grad_left.reshape(2, H, A),
        grad_right.reshape(4, H, B),
    )


def solution(mesh):
    specs = (P("seq", None, "chan"),) * 4 + (P(("seq", "chan"), None, None),) * 2
    return jax.shard_map(on_device, mesh=mesh, in_specs=specs, out_specs=specs, check_vma=False)
```

```python
import functools
import math

import jax
import jax.numpy as jnp
from jax import lax
from jax.experimental import pallas as pl
from jax.experimental.pallas import tpu as pltpu
from jax.sharding import PartitionSpec as P

MESH = pl.DeviceIdType.MESH
BF = jnp.bfloat16
F32 = jnp.float32
A = 256
B = 512
C = 1536
H = 8
LANE = 128
SEQ = 32
RIGHT_PARTS = ((0, 256, (0, 1, 2)), (256, 128, (1, 2, 0)), (384, 128, (2, 0, 1)))


def place():
    seq = lax.axis_index("seq")
    chan = lax.axis_index("chan")
    x = ((seq // 4) % 2) * 2 + chan // 2
    return (x, seq // 8, seq % 4), chan % 2


def device_at(xyz, core):
    x, y, z = xyz
    return (y * 8 + (x // 2) * 4 + z, (x % 2) * 2 + core)


def moved(xyz, axis, step):
    new = list(xyz)
    new[axis] = (xyz[axis] + step) % 4
    return tuple(new)


def chip_friends(xyz, core):
    return [device_at(xyz, 1 - core)] + [
        device_at(moved(xyz, axis, step), core) for axis in range(3) for step in (1, 2, 3)
    ]


def remote(src, dst, send, recv, device):
    return pltpu.make_async_remote_copy(
        src_ref=src, dst_ref=dst, send_sem=send, recv_sem=recv, device_id=device, device_id_type=MESH
    )


def aligned(value, multiple):
    return pl.multiple_of(value, multiple)


def masks_of(rows):
    lane = lax.broadcasted_iota(jnp.int32, (rows, LANE), 1)
    return [(lane & bit) != 0 for bit in (1, 2, 4)]


def turn(values, masks):
    for bit, mask in zip((1, 2, 4), masks):
        values = [jnp.where(mask, values[(i + bit) % 8], values[i]) for i in range(8)]
    return values


def to_groups(values, masks):
    values = turn([v if n == 0 else pltpu.roll(v, n, 1) for n, v in enumerate(values)], masks)
    return [values[(-h) % 8] for h in range(8)]


def from_groups(values, masks):
    values = turn(values, masks)
    return [values[0]] + [pltpu.roll(values[(-n) % 8], LANE - n, 1) for n in range(1, 8)]


def dot(a, b, ca, cb):
    return lax.dot_general(a, b, (((ca,), (cb,)), ((), ())), preferred_element_type=F32)


def seq_offset(k):
    return (k * 7) % SEQ


def seq_moved(seq, off):
    y, xh, z = seq // 8, (seq // 4) % 2, seq % 4
    dy, dx, dz = off // 8, (off // 4) % 2, off % 4
    return ((y + dy) % 4) * 8 + ((xh + dx) % 2) * 4 + (z + dz) % 4


class Exchange:
    def __init__(self, src, dst, send, recv, local):
        self.src, self.dst, self.send, self.recv, self.local = src, dst, send, recv, local

    def copy(self, j, k):
        me = lax.axis_index("seq")
        peer = seq_moved(me, seq_offset(k))
        lanes = pl.ds(j * LANE, LANE)
        return remote(
            self.src.at[:, pl.ds(aligned(peer * 16, 16), 16), lanes],
            self.dst.at[:, pl.ds(aligned(me * 16, 16), 16), lanes],
            self.send.at[j, k],
            self.recv.at[j, k],
            (peer, lax.axis_index("chan")),
        )

    def own(self, j):
        rows = pl.ds(aligned(lax.axis_index("seq") * 16, 16), 16)
        lanes = pl.ds(j * LANE, LANE)
        return pltpu.make_async_copy(self.src.at[:, rows, lanes], self.dst.at[:, rows, lanes], self.local.at[j])

    def start(self, j):
        def step(k, _):
            self.copy(j, k).start()
            return _

        lax.fori_loop(1, SEQ, step, 0)
        self.own(j).start()

    def arrived(self, j):
        def step(k, _):
            self.copy(j, k).wait_recv()
            return _

        self.own(j).wait()
        lax.fori_loop(1, SEQ, step, 0)

    def sent(self, j):
        def step(k, _):
            self.copy(j, k).wait_send()
            return _

        lax.fori_loop(1, SEQ, step, 0)


class Gather:
    def __init__(self, buf, rows, lane, lanes, order, send, recv):
        self.buf, self.rows, self.lanes, self.order = buf, rows, pl.ds(lane, lanes), order
        self.send, self.recv = send, recv

    def copies(self, stage):
        xyz, core = place()
        index = tuple(slice(None) if axis in self.order[:stage] else xyz[axis] for axis in range(3))
        ref = self.buf.at[index + (pl.ds(aligned(core * self.rows, self.rows), self.rows), self.lanes)]
        return [
            remote(
                ref,
                ref,
                self.send.at[stage, step - 1],
                self.recv.at[stage, step - 1],
                device_at(moved(xyz, self.order[stage], step), core),
            )
            for step in (1, 2, 3)
        ]

    def start(self, stage):
        for copy in self.copies(stage):
            copy.start()

    def wait(self, stage):
        for copy in self.copies(stage):
            copy.wait()


class Reduce:
    def __init__(self, buf, heaps, out, scale, lane, lanes, order, send, recv):
        self.buf, self.heaps, self.out, self.scale = buf, heaps, out, scale
        self.lanes, self.order, self.send, self.recv = pl.ds(lane, lanes), order, send, recv

    def copies(self, stage):
        xyz, core = place()
        axis = self.order[stage]
        found = []
        for step in (1, 2, 3):
            to = moved(xyz, axis, step)
            index = tuple(slice(None) if n in self.order[stage + 1 :] else to[n] for n in range(3))
            found.append(
                remote(
                    self.buf.at[index + (slice(None), self.lanes)],
                    self.heaps[stage].at[(step - 1,) + (slice(None),) * (3 - stage) + (self.lanes,)],
                    self.send.at[stage, step - 1],
                    self.recv.at[stage, step - 1],
                    device_at(to, core),
                )
            )
        return found

    def start(self, stage):
        for copy in self.copies(stage):
            copy.start()

    def finish(self, stage):
        for copy in self.copies(stage):
            copy.wait()
        xyz, _ = place()
        rest = sorted(self.order[stage + 1 :])

        def one(i, carry):
            at = list(xyz)
            spots = [i // 4, i % 4][2 - len(rest) :]
            for axis, spot in zip(rest, spots):
                at[axis] = spot
            index = (*at, slice(None), self.lanes)
            value = self.buf[index].astype(F32)
            for step in range(3):
                value = value + self.heaps[stage][(step, *spots, slice(None), self.lanes)].astype(F32)
            if stage == 2:
                self.out[:, self.lanes] = value / self.scale
            else:
                self.buf[index] = value.astype(BF)
            return carry

        if rest:
            lax.fori_loop(0, 4 ** len(rest), one, 0)
        else:
            one(0, 0)


def plane_device(step):
    (x, y, z), core = place()
    return device_at((x, (y + step // 4) % 4, (z + step % 4) % 4), core)


class PlaneGather:
    def __init__(self, buf, lane, plane_first, axis_sems, plane_sems):
        self.buf, self.lanes, self.plane_first = buf, pl.ds(lane, LANE), plane_first
        self.axis_sems, self.plane_sems = axis_sems, plane_sems

    def ref(self, stage):
        (x, y, z), core = place()
        spot = (x, y, z) if stage == 0 else (x, slice(None), slice(None)) if self.plane_first else (slice(None), y, z)
        return self.buf.at[spot + (pl.ds(aligned(core * 16, 16), 16), self.lanes)]

    def each(self, stage, act):
        ref = self.ref(stage)
        if self.plane_first == (stage == 0):

            def one(step, carry):
                act(remote(ref, ref, self.plane_sems.at[0, step], self.plane_sems.at[1, step], plane_device(step)))
                return carry

            lax.fori_loop(1, 16, one, 0)
        else:
            xyz, core = place()
            for step in (1, 2, 3):
                device = device_at(moved(xyz, 0, step), core)
                act(remote(ref, ref, self.axis_sems.at[0, step], self.axis_sems.at[1, step], device))

    def start(self, stage):
        self.each(stage, lambda copy: copy.start())

    def wait(self, stage):
        self.each(stage, lambda copy: copy.wait())


class PlaneReduce:
    def __init__(self, buf, heaps, out, scale, lane, axis_first, axis_sems, plane_sems):
        self.buf, self.heaps, self.out, self.scale = buf, heaps, out, scale
        self.lanes, self.axis_first = pl.ds(lane, LANE), axis_first
        self.axis_sems, self.plane_sems = axis_sems, plane_sems

    def each(self, stage, act):
        (x, y, z), core = place()
        heap = self.heaps[stage]
        if self.axis_first == (stage == 0):
            spots = (slice(None), slice(None)) if stage == 0 else (y, z)
            for step in (1, 2, 3):
                to = (x + step) % 4
                src = self.buf.at[(to,) + spots + (slice(None), self.lanes)]
                sems = self.axis_sems.at[0, step], self.axis_sems.at[1, step]
                act(remote(src, heap.at[step - 1], *sems, device_at((to, y, z), core)))
        else:
            spot = slice(None) if stage == 0 else x

            def one(step, carry):
                src = self.buf.at[spot, (y + step // 4) % 4, (z + step % 4) % 4, :, self.lanes]
                sems = self.plane_sems.at[0, step], self.plane_sems.at[1, step]
                act(remote(src, heap.at[step - 1], *sems, plane_device(step)))
                return carry

            lax.fori_loop(1, 16, one, 0)

    def start(self, stage):
        self.each(stage, lambda copy: copy.start())

    def finish(self, stage):
        self.each(stage, lambda copy: copy.wait())
        (x, y, z), _ = place()
        heap = self.heaps[stage]
        count = 3 if self.axis_first == (stage == 0) else 15

        def total(index, spots):
            value = self.buf[(*index, slice(None), self.lanes)].astype(F32)
            for step in range(count):
                value = value + heap[(step, *spots)].astype(F32)
            return value

        if stage == 1:
            self.out[:, self.lanes] = total((x, y, z), ()) / self.scale
        elif self.axis_first:

            def one(i, carry):
                self.buf[x, i // 4, i % 4, :, self.lanes] = total((x, i // 4, i % 4), (i // 4, i % 4)).astype(BF)
                return carry

            lax.fori_loop(0, 16, one, 0)
        else:
            for n in range(4):
                self.buf[n, y, z, :, self.lanes] = total((n, y, z), (n,)).astype(BF)


def blocks(body, j):
    def step(i, _):
        body(i, aligned(i * 16, 16), slice(j * LANE, (j + 1) * LANE))
        return _

    lax.fori_loop(0, 32, step, 0)


def chip_of(seq):
    return ((seq // 4) % 2) * 2, seq // 8, seq % 4


def layer_kernel(
    in_ref, gate_ref, ker_ref, cot_ref, right_ref, left_ref,
    out_ref, gin_ref, ggate_ref, gker_ref, gleft_ref, gright_ref,
    out, xin, xgate, xker, cot, gated, bsend, brecv, tsend, trecv, right, left, work, gsum, piece, raw_r, raw_l,
    own_r, sib_r, got_r, d0_r, d1_r, d2_r, own_l, sib_l, got_l, a0_l, a1_l, b0_l, b1_l,
    load, own, sems, stores, core_sems, gather_sems, reduce_sems, axis_sems, plane_sems,
):
    me = lax.axis_index("seq")
    chan = lax.axis_index("chan")
    xyz, core = place()
    sibling = device_at(xyz, 1 - core)
    barrier = pltpu.get_barrier_semaphore()
    tgrp = bsend

    loads = {
        "cot0": pltpu.make_async_copy(cot_ref.at[pl.ds(0, 8)], cot.at[:, pl.ds(0, 256), :], load.at[0]),
        "cot1": pltpu.make_async_copy(cot_ref.at[pl.ds(8, 8)], cot.at[:, pl.ds(256, 256), :], load.at[1]),
        "in": pltpu.make_async_copy(in_ref, xin, load.at[2]),
        "gate": pltpu.make_async_copy(gate_ref, xgate, load.at[3]),
        "ker": pltpu.make_async_copy(ker_ref, xker, load.at[4]),
        "left": pltpu.make_async_copy(
            left_ref, raw_l.at[(*xyz, pl.ds(aligned(core * 16, 16), 16))], load.at[5]
        ),
        "right": pltpu.make_async_copy(
            right_ref, raw_r.at[(*xyz, pl.ds(aligned(core * 32, 32), 32))], load.at[6]
        ),
    }

    def hello(k, _):
        pl.semaphore_signal(barrier, inc=1, device_id=(seq_moved(me, seq_offset(k)), chan), device_id_type=MESH)
        return _

    lax.fori_loop(1, SEQ, hello, 0)
    friends = chip_friends(xyz, core)
    for device in friends:
        pl.semaphore_signal(barrier, inc=1, device_id=device, device_id_type=MESH)
    for name in ("left", "right", "cot0", "cot1"):
        loads[name].start()
    pl.semaphore_wait(barrier, SEQ - 1 + len(friends))
    loads["left"].wait()
    loads["right"].wait()
    masks = masks_of(16)

    gather_l = [
        PlaneGather(raw_l, 0, True, axis_sems.at[0], plane_sems.at[0]),
        PlaneGather(raw_l, LANE, False, axis_sems.at[1], plane_sems.at[1]),
    ]
    gather_r = [
        Gather(raw_r, 32, *part, gather_sems.at[0, n], gather_sems.at[1, n])
        for n, part in enumerate(RIGHT_PARTS)
    ]
    mine_l = raw_l.at[:, :, :, pl.ds(aligned(core * 16, 16), 16), :]
    mine_r = raw_r.at[:, :, :, pl.ds(aligned(core * 32, 32), 32), :]
    swap_l = remote(mine_l, mine_l, core_sems.at[0, 0], core_sems.at[1, 0], sibling)
    swap_r = remote(mine_r, mine_r, core_sems.at[0, 1], core_sems.at[1, 1], sibling)
    back = Exchange(bsend, brecv, sems.at[0], sems.at[1], own.at[0])
    twisted = Exchange(tsend, trecv, sems.at[2], sems.at[3], own.at[1])

    def cot_groups(i, row, lanes):
        values = [cot[n, pl.ds(row, 16), lanes].astype(F32) for n in range(8)]
        for h, value in enumerate(to_groups(values, masks)):
            cot[h, pl.ds(row, 16), lanes] = value.astype(BF)

    for part in gather_l + gather_r:
        part.start(0)
    loads["cot0"].wait()
    loads["cot1"].wait()
    blocks(cot_groups, 0)
    for part in gather_l:
        part.wait(0)
        part.start(1)
    for part in gather_r:
        part.wait(0)
        part.start(1)
    for name in ("in", "gate", "ker"):
        loads[name].start()
    blocks(cot_groups, 1)
    blocks(cot_groups, 2)
    for part in gather_l:
        part.wait(1)
    swap_l.start()
    for part in gather_r:
        part.wait(1)
        part.start(2)
    swap_l.wait()

    def left_rows(pair, _):
        cx, cy, cz = chip_of(pair * 2)
        for lane in range(2):
            lanes = slice(lane * LANE, (lane + 1) * LANE)
            for n in range(4):
                piece[lane, n * 32 : n * 32 + 32, :] = raw_l[cx + n % 2, cy, cz + n // 2, :, lanes].astype(F32)
            for h in range(H):
                left[h, pl.ds(aligned(pair * 16, 16), 16), lanes] = piece[lane, pl.ds(h, 16, stride=8), :].astype(BF)
        return _

    lax.fori_loop(0, 16, left_rows, 0)

    def both(ref, h, lanes):
        return jnp.concatenate([ref[h, :256, lanes], ref[h, 256:, lanes]], axis=1)

    def back_rows(j):
        lanes = slice(j * LANE, (j + 1) * LANE)

        def product(h, _):
            value = dot(left[h], both(cot, h, lanes), 0, 0)
            work[j, pl.ds(aligned(h * 512, 512), 256), :] = value[:, :LANE]
            work[j, pl.ds(aligned(h * 512 + 256, 256), 256), :] = value[:, LANE:]
            return _

        lax.fori_loop(0, H, product, 0)

        def rows(i, _):
            for half in range(2):
                values = [work[j, pl.ds(aligned(h * 512 + half * 256 + i * 16, 16), 16), :] for h in range(8)]
                for n, value in enumerate(from_groups(values, masks)):
                    piece[j, pl.ds(half * 8 + n, 16, stride=16), :] = value
            for k in range(16):
                to = aligned((2 * i + k // 8) * 16, 16)
                bsend[k % 8, pl.ds(to, 16), lanes] = piece[j, k * 16 : k * 16 + 16, :].astype(BF)
            return _

        lax.fori_loop(0, 16, rows, 0)

    for j in range(3):
        back_rows(j)
        back.start(j)

    loads["in"].wait()
    loads["gate"].wait()

    def gate_groups(i, row, lanes):
        rows = pl.ds(row, 16)
        values = [xin[n, rows, lanes].astype(F32) * xgate[n, rows, lanes].astype(F32) for n in range(8)]
        for h, value in enumerate(to_groups(values, masks)):
            gated[h, rows, lanes] = value.astype(BF)

    for j in range(3):
        blocks(gate_groups, j)
    for part in gather_r:
        part.wait(2)
    swap_r.start()
    loads["ker"].wait()
    swap_r.wait()

    def right_rows(seq, _):
        cx, cy, cz = chip_of(seq)
        for lane in range(4):
            lanes = slice(lane * LANE, (lane + 1) * LANE)
            for lo in range(2):
                piece[lane, lo * 64 : lo * 64 + 64, :] = raw_r[cx + lo, cy, cz, :, lanes].astype(F32)
            for h in range(H):
                right[h, pl.ds(aligned(seq * 16, 16), 16), lanes] = piece[lane, pl.ds(h, 16, stride=8), :].astype(BF)
        return _

    lax.fori_loop(0, 32, right_rows, 0)

    def spread(h, value):
        for j in range(3):
            work[j, pl.ds(aligned(h * 512, 512), 512), :] = value[:, j * LANE : (j + 1) * LANE]

    def inner_dot(h, _):
        spread(h, dot(right[h], gated[h], 1, 0))
        return _

    lax.fori_loop(0, H, inner_dot, 0)

    def group_rows(j, row):
        return [work[j, pl.ds(aligned(h * 512 + row, 16), 16), :] for h in range(8)]

    def twist(j):
        def body(i, row, lanes):
            rows = pl.ds(row, 16)
            for n, value in enumerate(from_groups(group_rows(j, row), masks)):
                work[j, pl.ds(aligned(n * 512 + row, 16), 16), :] = value
                tsend[n, rows, lanes] = (xker[n, rows, lanes].astype(F32) * value).astype(BF)

        blocks(body, j)

    def push(j):
        def body(i, row, lanes):
            rows = pl.ds(row, 16)
            values = []
            spectral = group_rows(j, row)
            for n in range(8):
                value = brecv[n, rows, lanes].astype(F32)
                weight = xker[n, rows, lanes].astype(F32)
                xker[n, rows, lanes] = (value * spectral[n]).astype(BF)
                values.append(weight * value)
            for h, value in enumerate(to_groups(values, masks)):
                brecv[h, rows, lanes] = value.astype(BF)

        blocks(body, j)

    for j in range(3):
        twist(j)
    for j in range(3):
        back.arrived(j)
        twisted.start(j)
        push(j)

    save = [pltpu.make_async_copy(xker, gker_ref, stores.at[0])]
    save[0].start()

    def pack_right(block):
        def product(h, _):
            value = dot(brecv[h, block * 128 : block * 128 + 128, :], gated[h], 1, 1)
            for lane in range(4):
                row = aligned(h * 512 + lane * 128, 128)
                work[0, pl.ds(row, 128), :] = value[:, lane * LANE : (lane + 1) * LANE]
            return _

        lax.fori_loop(0, H, product, 0)

        def rows(n, _):
            cx, cy, cz = chip_of(block * 8 + n)
            for lane in range(4):
                lanes = slice(lane * LANE, (lane + 1) * LANE)
                for lo in range(2):
                    for buf, which in ((sib_r, 1 - core), (own_r, core)):
                        row = lane * 128 + n * 16 + lo * 8 + which * 4
                        for half in range(2):
                            tile = jnp.concatenate(
                                [work[0, pl.ds(row + half * 2 + r, 8, stride=512), :] for r in range(2)], axis=0
                            )
                            buf[cx + lo, cy, cz, half * 16 : half * 16 + 16, lanes] = tile.astype(BF)
            return _

        lax.fori_loop(0, 8, rows, 0)

    for block in range(4):
        pack_right(block)
    pair_r = remote(sib_r, got_r, core_sems.at[0, 2], core_sems.at[1, 2], sibling)
    pair_r.start()
    reduce_r = [
        Reduce(own_r, (d0_r, d1_r, d2_r), gright_ref, math.sqrt(A * C / H), *part, reduce_sems.at[0, n], reduce_sems.at[1, n])
        for n, part in enumerate(RIGHT_PARTS)
    ]
    reduce_l = [
        PlaneReduce(own_l, (a0_l, a1_l), gleft_ref, math.sqrt(B * C / H), 0, True, axis_sems.at[2], plane_sems.at[2]),
        PlaneReduce(own_l, (b0_l, b1_l), gleft_ref, math.sqrt(B * C / H), LANE, False, axis_sems.at[3], plane_sems.at[3]),
    ]

    def gated_dot(h, _):
        spread(h, dot(right[h], brecv[h], 0, 0))
        return _

    lax.fori_loop(0, H, gated_dot, 0)
    pair_r.wait()

    def add_pair(i, _):
        index = (i // 16, (i // 4) % 4, i % 4)
        own_r[index] = (own_r[index].astype(F32) + got_r[index].astype(F32)).astype(BF)
        return _

    lax.fori_loop(0, 64, add_pair, 0)
    for part in reduce_r:
        part.start(0)

    def gate_grads(j):
        def body(i, row, lanes):
            rows = pl.ds(row, 16)
            for n, value in enumerate(from_groups(group_rows(j, row), masks)):
                first = xin[n, rows, lanes].astype(F32)
                second = xgate[n, rows, lanes].astype(F32)
                xin[n, rows, lanes] = (value * second).astype(BF)
                xgate[n, rows, lanes] = (value * first).astype(BF)

        blocks(body, j)

    for j in range(3):
        gate_grads(j)
    save.append(pltpu.make_async_copy(xin, gin_ref, stores.at[1]))
    save.append(pltpu.make_async_copy(xgate, ggate_ref, stores.at[2]))
    save[1].start()
    save[2].start()
    for j in range(3):
        back.sent(j)

    def twist_groups(j):
        lanes = slice(j * LANE, (j + 1) * LANE)

        def rows(i, _):
            for k in range(16):
                at = aligned((2 * i + k // 8) * 16, 16)
                piece[j, k * 16 : k * 16 + 16, :] = trecv[k % 8, pl.ds(at, 16), lanes].astype(F32)
            for half in range(2):
                values = [piece[j, pl.ds(half * 8 + n, 16, stride=16), :] for n in range(8)]
                for h, value in enumerate(to_groups(values, masks)):
                    tgrp[h, pl.ds(aligned(half * 256 + i * 16, 16), 16), lanes] = value.astype(BF)
            return _

        lax.fori_loop(0, 16, rows, 0)

    def left_terms(j):
        lanes = slice(j * LANE, (j + 1) * LANE)

        def product(h, _):
            value = dot(both(cot, h, lanes), both(tgrp, h, lanes), 1, 1)
            rows = pl.ds(aligned(h * 256, 256), 256)
            for lane in range(2):
                term = value[:, lane * LANE : (lane + 1) * LANE]
                gsum[lane, rows, :] = term if j == 0 else gsum[lane, rows, :] + term
            return _

        lax.fori_loop(0, H, product, 0)

    def outer(j):
        lanes = slice(j * LANE, (j + 1) * LANE)

        def product(h, _):
            value = dot(left[h], both(tgrp, h, lanes), 1, 0)
            work[j, pl.ds(aligned(h * 512, 512), 256), :] = value[:, :LANE]
            work[j, pl.ds(aligned(h * 512 + 256, 256), 256), :] = value[:, LANE:]
            return _

        lax.fori_loop(0, H, product, 0)

        def body(i, row, lanes):
            for n, value in enumerate(from_groups(group_rows(j, row), masks)):
                out[(i // 16) * 8 + n, pl.ds(aligned((i % 16) * 16, 16), 16), lanes] = value.astype(BF)

        blocks(body, j)

    for j in range(3):
        twisted.arrived(j)
        twist_groups(j)
        left_terms(j)
        if j == 1:
            for part in reduce_r:
                part.finish(0)
                part.start(1)

    def left_tile(seq, lo, which, lane):
        row = seq * 8 + lo * 4 + which * 2
        return jnp.concatenate([gsum[lane, pl.ds(row + r, 8, stride=256), :] for r in range(2)], axis=0)

    def pack_left(seq, _):
        cx, cy, cz = chip_of(seq)
        for lo in range(2):
            for lane in range(2):
                lanes = slice(lane * LANE, (lane + 1) * LANE)
                sib_l[cx + lo, cy, cz, :, lanes] = left_tile(seq, lo, 1 - core, lane).astype(BF)
        return _

    def add_left(seq, _):
        cx, cy, cz = chip_of(seq)
        for lo in range(2):
            for lane in range(2):
                lanes = slice(lane * LANE, (lane + 1) * LANE)
                value = left_tile(seq, lo, core, lane) + got_l[cx + lo, cy, cz, :, lanes].astype(F32)
                own_l[cx + lo, cy, cz, :, lanes] = value.astype(BF)
        return _

    lax.fori_loop(0, SEQ, pack_left, 0)
    pair_l = remote(sib_l, got_l, core_sems.at[0, 3], core_sems.at[1, 3], sibling)
    pair_l.start()
    outer(0)
    pair_l.wait()
    lax.fori_loop(0, SEQ, add_left, 0)
    for part in reduce_l:
        part.start(0)
    for part in reduce_r:
        part.finish(1)
        part.start(2)
    outer(1)
    for part in reduce_l:
        part.finish(0)
        part.start(1)
    outer(2)
    save.append(pltpu.make_async_copy(out, out_ref, stores.at[3]))
    save[3].start()
    for part in reduce_r:
        part.finish(2)
    for part in reduce_l:
        part.finish(1)
    for j in range(3):
        twisted.sent(j)
    for copy in save:
        copy.wait()


def layer(inputs, gate_values, kernel, grad_out, right, left):
    hbm = pl.BlockSpec(memory_space=pl.ANY)
    vmem = pl.BlockSpec(memory_space=pltpu.VMEM)
    rows = pltpu.VMEM((8, B, 384), BF)

    return pl.pallas_call(
        layer_kernel,
        out_shape=(
            jax.ShapeDtypeStruct((16, A, 384), BF),
            jax.ShapeDtypeStruct((8, B, 384), BF),
            jax.ShapeDtypeStruct((8, B, 384), BF),
            jax.ShapeDtypeStruct((8, B, 384), BF),
            jax.ShapeDtypeStruct((16, A), F32),
            jax.ShapeDtypeStruct((32, B), F32),
        ),
        in_specs=[hbm] * 6,
        out_specs=(hbm,) * 4 + (vmem,) * 2,
        scratch_shapes=[pltpu.VMEM((16, A, 384), BF)]
        + [rows] * 9
        + [
            pltpu.VMEM((H, B, B), BF),
            pltpu.VMEM((H, A, A), BF),
            pltpu.VMEM((3, H * B, LANE), F32),
            pltpu.VMEM((2, H * A, LANE), F32),
            pltpu.VMEM((4, 256, LANE), F32),
            pltpu.VMEM((4, 4, 4, 64, B), BF),
            pltpu.VMEM((4, 4, 4, 32, A), BF),
        ]
        + [pltpu.VMEM((4, 4, 4, 32, B), BF)] * 3
        + [pltpu.VMEM((3,) + (4,) * n + (32, B), BF) for n in (2, 1, 0)]
        + [pltpu.VMEM((4, 4, 4, 16, A), BF)] * 3
        + [
            pltpu.VMEM((3, 4, 4, 16, LANE), BF),
            pltpu.VMEM((15, 16, LANE), BF),
            pltpu.VMEM((15, 4, 16, LANE), BF),
            pltpu.VMEM((3, 16, LANE), BF),
            pltpu.SemaphoreType.DMA((7,)),
            pltpu.SemaphoreType.DMA((2, 3)),
            pltpu.SemaphoreType.DMA((4, 3, SEQ)),
            pltpu.SemaphoreType.DMA((4,)),
            pltpu.SemaphoreType.DMA((2, 4)),
            pltpu.SemaphoreType.DMA((2, 3, 3, 3)),
            pltpu.SemaphoreType.DMA((2, 3, 3, 3)),
            pltpu.SemaphoreType.DMA((4, 2, 4)),
            pltpu.SemaphoreType.DMA((4, 2, 16)),
        ],
        compiler_params=pltpu.CompilerParams(collective_id=0, has_side_effects=True, vmem_limit_bytes=60 << 20),
        name="layer",
    )(inputs, gate_values, kernel, grad_out, right, left)


def on_device(inputs, gate_values, kernel, grad_out, left_tiles, right_tiles):
    output, grad_inputs, grad_gates, grad_kernel, grad_left, grad_right = layer(
        inputs, gate_values, kernel, grad_out, right_tiles.reshape(32, B), left_tiles.reshape(16, A)
    )
    return (
        output,
        grad_inputs,
        grad_gates,
        grad_kernel,
        grad_left.reshape(2, H, A),
        grad_right.reshape(4, H, B),
    )


def solution(mesh):
    specs = (P("seq", None, "chan"),) * 4 + (P(("seq", "chan"), None, None),) * 2
    return jax.shard_map(on_device, mesh=mesh, in_specs=specs, out_specs=specs, check_vma=False)
```

```python
import functools
import math

import jax
import jax.numpy as jnp
from jax import lax
from jax.experimental import pallas as pl
from jax.experimental.pallas import tpu as pltpu
from jax.sharding import PartitionSpec as P

MESH = pl.DeviceIdType.MESH
BF = jnp.bfloat16
F32 = jnp.float32
A = 256
B = 512
C = 1536
H = 8
LANE = 128
SEQ = 32
RIGHT_PARTS = ((0, 16, 0, 384, (0, 1, 2)), (16, 16, 0, 384, (1, 2, 0)), (0, 32, 384, 128, (2, 0, 1)))


def place():
    seq = lax.axis_index("seq")
    chan = lax.axis_index("chan")
    x = ((seq // 4) % 2) * 2 + chan // 2
    return (x, seq // 8, seq % 4), chan % 2


def device_at(xyz, core):
    x, y, z = xyz
    return (y * 8 + (x // 2) * 4 + z, (x % 2) * 2 + core)


def moved(xyz, axis, step):
    new = list(xyz)
    new[axis] = (xyz[axis] + step) % 4
    return tuple(new)


def chip_friends(xyz, core):
    return [device_at(xyz, 1 - core)] + [
        device_at(moved(xyz, axis, step), core) for axis in range(3) for step in (1, 2, 3)
    ]


def remote(src, dst, send, recv, device):
    return pltpu.make_async_remote_copy(
        src_ref=src, dst_ref=dst, send_sem=send, recv_sem=recv, device_id=device, device_id_type=MESH
    )


def aligned(value, multiple):
    return pl.multiple_of(value, multiple)


def masks_of(rows):
    lane = lax.broadcasted_iota(jnp.int32, (rows, LANE), 1)
    return [(lane & bit) != 0 for bit in (1, 2, 4)]


def turn(values, masks):
    for bit, mask in zip((1, 2, 4), masks):
        values = [jnp.where(mask, values[(i + bit) % 8], values[i]) for i in range(8)]
    return values


def to_groups(values, masks):
    values = turn([v if n == 0 else pltpu.roll(v, n, 1) for n, v in enumerate(values)], masks)
    return [values[(-h) % 8] for h in range(8)]


def from_groups(values, masks):
    values = turn(values, masks)
    return [values[0]] + [pltpu.roll(values[(-n) % 8], LANE - n, 1) for n in range(1, 8)]


def dot(a, b, ca, cb):
    return lax.dot_general(a, b, (((ca,), (cb,)), ((), ())), preferred_element_type=F32)


def seq_offset(k):
    return (k * 7) % SEQ


def seq_moved(seq, off):
    y, xh, z = seq // 8, (seq // 4) % 2, seq % 4
    dy, dx, dz = off // 8, (off // 4) % 2, off % 4
    return ((y + dy) % 4) * 8 + ((xh + dx) % 2) * 4 + (z + dz) % 4


class Exchange:
    def __init__(self, src, dst, send, recv, local):
        self.src, self.dst, self.send, self.recv, self.local = src, dst, send, recv, local

    def copy(self, j, k):
        me = lax.axis_index("seq")
        peer = seq_moved(me, seq_offset(k))
        lanes = pl.ds(j * LANE, LANE)
        return remote(
            self.src.at[:, pl.ds(aligned(peer * 16, 16), 16), lanes],
            self.dst.at[:, pl.ds(aligned(me * 16, 16), 16), lanes],
            self.send.at[j, k],
            self.recv.at[j, k],
            (peer, lax.axis_index("chan")),
        )

    def own(self, j):
        rows = pl.ds(aligned(lax.axis_index("seq") * 16, 16), 16)
        lanes = pl.ds(j * LANE, LANE)
        return pltpu.make_async_copy(self.src.at[:, rows, lanes], self.dst.at[:, rows, lanes], self.local.at[j])

    def start(self, j):
        def step(k, _):
            self.copy(j, k).start()
            return _

        lax.fori_loop(1, SEQ, step, 0)
        self.own(j).start()

    def arrived(self, j):
        def step(k, _):
            self.copy(j, k).wait_recv()
            return _

        self.own(j).wait()
        lax.fori_loop(1, SEQ, step, 0)

    def sent(self, j):
        def step(k, _):
            self.copy(j, k).wait_send()
            return _

        lax.fori_loop(1, SEQ, step, 0)


class Gather:
    def __init__(self, buf, row, rows, lane, lanes, order, send, recv):
        self.buf, self.row, self.rows, self.lanes, self.order = buf, row, rows, pl.ds(lane, lanes), order
        self.send, self.recv = send, recv

    def copies(self, stage):
        xyz, core = place()
        index = tuple(slice(None) if axis in self.order[:stage] else xyz[axis] for axis in range(3))
        ref = self.buf.at[index + (pl.ds(aligned(core * 32 + self.row, 16), self.rows), self.lanes)]
        return [
            remote(
                ref,
                ref,
                self.send.at[stage, step - 1],
                self.recv.at[stage, step - 1],
                device_at(moved(xyz, self.order[stage], step), core),
            )
            for step in (1, 2, 3)
        ]

    def start(self, stage):
        for copy in self.copies(stage):
            copy.start()

    def wait(self, stage):
        for copy in self.copies(stage):
            copy.wait()


class Reduce:
    def __init__(self, buf, heaps, out, scale, row, rows, lane, lanes, order, send, recv):
        self.buf, self.heaps, self.out, self.scale = buf, heaps, out, scale
        self.rows, self.lanes = pl.ds(row, rows), pl.ds(lane, lanes)
        self.order, self.send, self.recv = order, send, recv

    def copies(self, stage):
        xyz, core = place()
        axis = self.order[stage]
        found = []
        for step in (1, 2, 3):
            to = moved(xyz, axis, step)
            index = tuple(slice(None) if n in self.order[stage + 1 :] else to[n] for n in range(3))
            found.append(
                remote(
                    self.buf.at[index + (self.rows, self.lanes)],
                    self.heaps[stage].at[(step - 1,) + (slice(None),) * (2 - stage) + (self.rows, self.lanes)],
                    self.send.at[stage, step - 1],
                    self.recv.at[stage, step - 1],
                    device_at(to, core),
                )
            )
        return found

    def start(self, stage):
        for copy in self.copies(stage):
            copy.start()

    def finish(self, stage):
        for copy in self.copies(stage):
            copy.wait()
        xyz, _ = place()
        rest = sorted(self.order[stage + 1 :])

        def one(i, carry):
            at = list(xyz)
            spots = [i // 4, i % 4][2 - len(rest) :]
            for axis, spot in zip(rest, spots):
                at[axis] = spot
            index = (*at, self.rows, self.lanes)
            value = self.buf[index].astype(F32)
            for step in range(3):
                value = value + self.heaps[stage][(step, *spots, self.rows, self.lanes)].astype(F32)
            if stage == 2:
                self.out[self.rows, self.lanes] = value / self.scale
            else:
                self.buf[index] = value.astype(BF)
            return carry

        if rest:
            lax.fori_loop(0, 4 ** len(rest), one, 0)
        else:
            one(0, 0)


def plane_device(step):
    (x, y, z), core = place()
    return device_at((x, (y + step // 4) % 4, (z + step % 4) % 4), core)


class PlaneGather:
    def __init__(self, buf, lane, plane_first, axis_sems, plane_sems):
        self.buf, self.lanes, self.plane_first = buf, pl.ds(lane, LANE), plane_first
        self.axis_sems, self.plane_sems = axis_sems, plane_sems

    def ref(self, stage):
        (x, y, z), core = place()
        spot = (x, y, z) if stage == 0 else (x, slice(None), slice(None)) if self.plane_first else (slice(None), y, z)
        return self.buf.at[spot + (pl.ds(aligned(core * 16, 16), 16), self.lanes)]

    def each(self, stage, act):
        ref = self.ref(stage)
        if self.plane_first == (stage == 0):

            def one(step, carry):
                act(remote(ref, ref, self.plane_sems.at[0, step], self.plane_sems.at[1, step], plane_device(step)))
                return carry

            lax.fori_loop(1, 16, one, 0)
        else:
            xyz, core = place()
            for step in (1, 2, 3):
                device = device_at(moved(xyz, 0, step), core)
                act(remote(ref, ref, self.axis_sems.at[0, step], self.axis_sems.at[1, step], device))

    def start(self, stage):
        self.each(stage, lambda copy: copy.start())

    def wait(self, stage):
        self.each(stage, lambda copy: copy.wait())


class PlaneReduce:
    def __init__(self, buf, heaps, out, scale, lane, axis_first, axis_sems, plane_sems):
        self.buf, self.heaps, self.out, self.scale = buf, heaps, out, scale
        self.lanes, self.axis_first = pl.ds(lane, LANE), axis_first
        self.axis_sems, self.plane_sems = axis_sems, plane_sems

    def each(self, stage, act):
        (x, y, z), core = place()
        heap = self.heaps[stage]
        if self.axis_first == (stage == 0):
            spots = (slice(None), slice(None)) if stage == 0 else (y, z)
            for step in (1, 2, 3):
                to = (x + step) % 4
                src = self.buf.at[(to,) + spots + (slice(None), self.lanes)]
                sems = self.axis_sems.at[0, step], self.axis_sems.at[1, step]
                act(remote(src, heap.at[step - 1], *sems, device_at((to, y, z), core)))
        else:
            spot = slice(None) if stage == 0 else x

            def one(step, carry):
                src = self.buf.at[spot, (y + step // 4) % 4, (z + step % 4) % 4, :, self.lanes]
                sems = self.plane_sems.at[0, step], self.plane_sems.at[1, step]
                act(remote(src, heap.at[step - 1], *sems, plane_device(step)))
                return carry

            lax.fori_loop(1, 16, one, 0)

    def start(self, stage):
        self.each(stage, lambda copy: copy.start())

    def finish(self, stage):
        self.each(stage, lambda copy: copy.wait())
        (x, y, z), _ = place()
        heap = self.heaps[stage]
        count = 3 if self.axis_first == (stage == 0) else 15

        def total(index, spots):
            value = self.buf[(*index, slice(None), self.lanes)].astype(F32)
            for step in range(count):
                value = value + heap[(step, *spots)].astype(F32)
            return value

        if stage == 1:
            self.out[:, self.lanes] = total((x, y, z), ()) / self.scale
        elif self.axis_first:

            def one(i, carry):
                self.buf[x, i // 4, i % 4, :, self.lanes] = total((x, i // 4, i % 4), (i // 4, i % 4)).astype(BF)
                return carry

            lax.fori_loop(0, 16, one, 0)
        else:
            for n in range(4):
                self.buf[n, y, z, :, self.lanes] = total((n, y, z), (n,)).astype(BF)


def blocks(body, j):
    def step(i, _):
        body(i, aligned(i * 16, 16), slice(j * LANE, (j + 1) * LANE))
        return _

    lax.fori_loop(0, 32, step, 0)


def chip_of(seq):
    return ((seq // 4) % 2) * 2, seq // 8, seq % 4


def layer_kernel(
    in_ref, gate_ref, ker_ref, cot_ref, right_ref, left_ref,
    out_ref, gin_ref, ggate_ref, gker_ref, gleft_ref, gright_ref,
    out, xin, xgate, xker, cot, gated, bsend, brecv, tsend, trecv, right, left, work, gsum, piece, raw_r, raw_l,
    own_r, sib_r, got_r, d0_r, d1_r, d2_r, own_l, sib_l, got_l, a0_l, a1_l, b0_l, b1_l,
    load, own, sems, stores, core_sems, gather_sems, reduce_sems, axis_sems, plane_sems,
):
    me = lax.axis_index("seq")
    chan = lax.axis_index("chan")
    xyz, core = place()
    sibling = device_at(xyz, 1 - core)
    barrier = pltpu.get_barrier_semaphore()
    tgrp = bsend

    loads = {
        "cot0": pltpu.make_async_copy(cot_ref.at[pl.ds(0, 8)], cot.at[:, pl.ds(0, 256), :], load.at[0]),
        "cot1": pltpu.make_async_copy(cot_ref.at[pl.ds(8, 8)], cot.at[:, pl.ds(256, 256), :], load.at[1]),
        "in": pltpu.make_async_copy(in_ref, xin, load.at[2]),
        "gate": pltpu.make_async_copy(gate_ref, xgate, load.at[3]),
        "ker": pltpu.make_async_copy(ker_ref, xker, load.at[4]),
        "left": pltpu.make_async_copy(
            left_ref, raw_l.at[(*xyz, pl.ds(aligned(core * 16, 16), 16))], load.at[5]
        ),
        "right": pltpu.make_async_copy(
            right_ref, raw_r.at[(*xyz, pl.ds(aligned(core * 32, 32), 32))], load.at[6]
        ),
    }

    def hello(k, _):
        pl.semaphore_signal(barrier, inc=1, device_id=(seq_moved(me, seq_offset(k)), chan), device_id_type=MESH)
        return _

    lax.fori_loop(1, SEQ, hello, 0)
    friends = chip_friends(xyz, core)
    for device in friends:
        pl.semaphore_signal(barrier, inc=1, device_id=device, device_id_type=MESH)
    for name in ("left", "right", "cot0", "cot1"):
        loads[name].start()
    pl.semaphore_wait(barrier, SEQ - 1 + len(friends))
    loads["left"].wait()
    loads["right"].wait()
    masks = masks_of(16)

    gather_l = [
        PlaneGather(raw_l, 0, True, axis_sems.at[0], plane_sems.at[0]),
        PlaneGather(raw_l, LANE, False, axis_sems.at[1], plane_sems.at[1]),
    ]
    gather_r = [
        Gather(raw_r, *part, gather_sems.at[0, n], gather_sems.at[1, n])
        for n, part in enumerate(RIGHT_PARTS)
    ]
    mine_l = raw_l.at[:, :, :, pl.ds(aligned(core * 16, 16), 16), :]
    mine_r = raw_r.at[:, :, :, pl.ds(aligned(core * 32, 32), 32), :]
    swap_l = remote(mine_l, mine_l, core_sems.at[0, 0], core_sems.at[1, 0], sibling)
    swap_r = remote(mine_r, mine_r, core_sems.at[0, 1], core_sems.at[1, 1], sibling)
    back = Exchange(bsend, brecv, sems.at[0], sems.at[1], own.at[0])
    twisted = Exchange(tsend, trecv, sems.at[2], sems.at[3], own.at[1])

    def cot_groups(i, row, lanes):
        values = [cot[n, pl.ds(row, 16), lanes].astype(F32) for n in range(8)]
        for h, value in enumerate(to_groups(values, masks)):
            cot[h, pl.ds(row, 16), lanes] = value.astype(BF)

    for part in gather_l + gather_r:
        part.start(0)
    loads["cot0"].wait()
    loads["cot1"].wait()
    blocks(cot_groups, 0)
    for part in gather_l:
        part.wait(0)
        part.start(1)
    for part in gather_r:
        part.wait(0)
        part.start(1)
    for name in ("in", "gate", "ker"):
        loads[name].start()
    blocks(cot_groups, 1)
    blocks(cot_groups, 2)
    for part in gather_l:
        part.wait(1)
    swap_l.start()
    for part in gather_r:
        part.wait(1)
        part.start(2)
    swap_l.wait()

    def left_rows(pair, _):
        cx, cy, cz = chip_of(pair * 2)
        for lane in range(2):
            lanes = slice(lane * LANE, (lane + 1) * LANE)
            for n in range(4):
                piece[lane, n * 32 : n * 32 + 32, :] = raw_l[cx + n % 2, cy, cz + n // 2, :, lanes].astype(F32)
            for h in range(H):
                left[h, pl.ds(aligned(pair * 16, 16), 16), lanes] = piece[lane, pl.ds(h, 16, stride=8), :].astype(BF)
        return _

    lax.fori_loop(0, 16, left_rows, 0)

    def both(ref, h, lanes):
        return jnp.concatenate([ref[h, :256, lanes], ref[h, 256:, lanes]], axis=1)

    def back_rows(j):
        lanes = slice(j * LANE, (j + 1) * LANE)

        def product(h, _):
            value = dot(left[h], both(cot, h, lanes), 0, 0)
            work[j, pl.ds(aligned(h * 512, 512), 256), :] = value[:, :LANE]
            work[j, pl.ds(aligned(h * 512 + 256, 256), 256), :] = value[:, LANE:]
            return _

        lax.fori_loop(0, H, product, 0)

        def rows(i, _):
            for half in range(2):
                values = [work[j, pl.ds(aligned(h * 512 + half * 256 + i * 16, 16), 16), :] for h in range(8)]
                for n, value in enumerate(from_groups(values, masks)):
                    piece[j, pl.ds(half * 8 + n, 16, stride=16), :] = value
            for k in range(16):
                to = aligned((2 * i + k // 8) * 16, 16)
                bsend[k % 8, pl.ds(to, 16), lanes] = piece[j, k * 16 : k * 16 + 16, :].astype(BF)
            return _

        lax.fori_loop(0, 16, rows, 0)

    for j in range(3):
        back_rows(j)
        back.start(j)

    loads["in"].wait()
    loads["gate"].wait()

    def gate_groups(i, row, lanes):
        rows = pl.ds(row, 16)
        values = [xin[n, rows, lanes].astype(F32) * xgate[n, rows, lanes].astype(F32) for n in range(8)]
        for h, value in enumerate(to_groups(values, masks)):
            gated[h, rows, lanes] = value.astype(BF)

    for j in range(3):
        blocks(gate_groups, j)
    for part in gather_r:
        part.wait(2)
    swap_r.start()
    loads["ker"].wait()
    swap_r.wait()

    def right_rows(seq, _):
        cx, cy, cz = chip_of(seq)
        for lane in range(4):
            lanes = slice(lane * LANE, (lane + 1) * LANE)
            for lo in range(2):
                piece[lane, lo * 64 : lo * 64 + 64, :] = raw_r[cx + lo, cy, cz, :, lanes].astype(F32)
            for h in range(H):
                right[h, pl.ds(aligned(seq * 16, 16), 16), lanes] = piece[lane, pl.ds(h, 16, stride=8), :].astype(BF)
        return _

    lax.fori_loop(0, 32, right_rows, 0)

    def spread(h, value):
        for j in range(3):
            work[j, pl.ds(aligned(h * 512, 512), 512), :] = value[:, j * LANE : (j + 1) * LANE]

    def inner_dot(h, _):
        spread(h, dot(right[h], gated[h], 1, 0))
        return _

    lax.fori_loop(0, H, inner_dot, 0)

    def group_rows(j, row):
        return [work[j, pl.ds(aligned(h * 512 + row, 16), 16), :] for h in range(8)]

    def twist(j):
        def body(i, row, lanes):
            rows = pl.ds(row, 16)
            for n, value in enumerate(from_groups(group_rows(j, row), masks)):
                work[j, pl.ds(aligned(n * 512 + row, 16), 16), :] = value
                tsend[n, rows, lanes] = (xker[n, rows, lanes].astype(F32) * value).astype(BF)

        blocks(body, j)

    def push(j):
        def body(i, row, lanes):
            rows = pl.ds(row, 16)
            values = []
            spectral = group_rows(j, row)
            for n in range(8):
                value = brecv[n, rows, lanes].astype(F32)
                weight = xker[n, rows, lanes].astype(F32)
                xker[n, rows, lanes] = (value * spectral[n]).astype(BF)
                values.append(weight * value)
            for h, value in enumerate(to_groups(values, masks)):
                brecv[h, rows, lanes] = value.astype(BF)

        blocks(body, j)

    for j in range(3):
        twist(j)
    for j in range(3):
        back.arrived(j)
        twisted.start(j)
        push(j)

    save = [pltpu.make_async_copy(xker, gker_ref, stores.at[0])]
    save[0].start()

    def pack_right(block):
        def product(h, _):
            value = dot(brecv[h, block * 128 : block * 128 + 128, :], gated[h], 1, 1)
            for lane in range(4):
                row = aligned(h * 512 + lane * 128, 128)
                work[0, pl.ds(row, 128), :] = value[:, lane * LANE : (lane + 1) * LANE]
            return _

        lax.fori_loop(0, H, product, 0)

        def rows(n, _):
            cx, cy, cz = chip_of(block * 8 + n)
            for lane in range(4):
                lanes = slice(lane * LANE, (lane + 1) * LANE)
                for lo in range(2):
                    for buf, which in ((sib_r, 1 - core), (own_r, core)):
                        row = lane * 128 + n * 16 + lo * 8 + which * 4
                        for half in range(2):
                            tile = jnp.concatenate(
                                [work[0, pl.ds(row + half * 2 + r, 8, stride=512), :] for r in range(2)], axis=0
                            )
                            buf[cx + lo, cy, cz, half * 16 : half * 16 + 16, lanes] = tile.astype(BF)
            return _

        lax.fori_loop(0, 8, rows, 0)

    for block in range(4):
        pack_right(block)
    pair_r = remote(sib_r, got_r, core_sems.at[0, 2], core_sems.at[1, 2], sibling)
    pair_r.start()
    reduce_r = [
        Reduce(own_r, (d0_r, d1_r, d2_r), gright_ref, math.sqrt(A * C / H), *part, reduce_sems.at[0, n], reduce_sems.at[1, n])
        for n, part in enumerate(RIGHT_PARTS)
    ]
    reduce_l = [
        PlaneReduce(own_l, (a0_l, a1_l), gleft_ref, math.sqrt(B * C / H), 0, True, axis_sems.at[2], plane_sems.at[2]),
        PlaneReduce(own_l, (b0_l, b1_l), gleft_ref, math.sqrt(B * C / H), LANE, False, axis_sems.at[3], plane_sems.at[3]),
    ]

    def gated_dot(h, _):
        spread(h, dot(right[h], brecv[h], 0, 0))
        return _

    lax.fori_loop(0, H, gated_dot, 0)
    pair_r.wait()

    def add_pair(i, _):
        index = (i // 16, (i // 4) % 4, i % 4)
        own_r[index] = (own_r[index].astype(F32) + got_r[index].astype(F32)).astype(BF)
        return _

    lax.fori_loop(0, 64, add_pair, 0)
    for part in reduce_r:
        part.start(0)

    def gate_grads(j):
        def body(i, row, lanes):
            rows = pl.ds(row, 16)
            for n, value in enumerate(from_groups(group_rows(j, row), masks)):
                first = xin[n, rows, lanes].astype(F32)
                second = xgate[n, rows, lanes].astype(F32)
                xin[n, rows, lanes] = (value * second).astype(BF)
                xgate[n, rows, lanes] = (value * first).astype(BF)

        blocks(body, j)

    for j in range(3):
        gate_grads(j)
    save.append(pltpu.make_async_copy(xin, gin_ref, stores.at[1]))
    save.append(pltpu.make_async_copy(xgate, ggate_ref, stores.at[2]))
    save[1].start()
    save[2].start()
    for j in range(3):
        back.sent(j)

    def twist_groups(j):
        lanes = slice(j * LANE, (j + 1) * LANE)

        def rows(i, _):
            for k in range(16):
                at = aligned((2 * i + k // 8) * 16, 16)
                piece[j, k * 16 : k * 16 + 16, :] = trecv[k % 8, pl.ds(at, 16), lanes].astype(F32)
            for half in range(2):
                values = [piece[j, pl.ds(half * 8 + n, 16, stride=16), :] for n in range(8)]
                for h, value in enumerate(to_groups(values, masks)):
                    tgrp[h, pl.ds(aligned(half * 256 + i * 16, 16), 16), lanes] = value.astype(BF)
            return _

        lax.fori_loop(0, 16, rows, 0)

    def left_terms(j):
        lanes = slice(j * LANE, (j + 1) * LANE)

        def product(h, _):
            value = dot(both(cot, h, lanes), both(tgrp, h, lanes), 1, 1)
            rows = pl.ds(aligned(h * 256, 256), 256)
            for lane in range(2):
                term = value[:, lane * LANE : (lane + 1) * LANE]
                gsum[lane, rows, :] = term if j == 0 else gsum[lane, rows, :] + term
            return _

        lax.fori_loop(0, H, product, 0)

    def outer(j):
        lanes = slice(j * LANE, (j + 1) * LANE)

        def product(h, _):
            value = dot(left[h], both(tgrp, h, lanes), 1, 0)
            work[j, pl.ds(aligned(h * 512, 512), 256), :] = value[:, :LANE]
            work[j, pl.ds(aligned(h * 512 + 256, 256), 256), :] = value[:, LANE:]
            return _

        lax.fori_loop(0, H, product, 0)

        def body(i, row, lanes):
            for n, value in enumerate(from_groups(group_rows(j, row), masks)):
                out[(i // 16) * 8 + n, pl.ds(aligned((i % 16) * 16, 16), 16), lanes] = value.astype(BF)

        blocks(body, j)

    for j in range(3):
        twisted.arrived(j)
        twist_groups(j)
        left_terms(j)

    def left_tile(seq, lo, which, lane):
        row = seq * 8 + lo * 4 + which * 2
        return jnp.concatenate([gsum[lane, pl.ds(row + r, 8, stride=256), :] for r in range(2)], axis=0)

    def pack_left(seq, _):
        cx, cy, cz = chip_of(seq)
        for lo in range(2):
            for lane in range(2):
                lanes = slice(lane * LANE, (lane + 1) * LANE)
                sib_l[cx + lo, cy, cz, :, lanes] = left_tile(seq, lo, 1 - core, lane).astype(BF)
        return _

    def add_left(seq, _):
        cx, cy, cz = chip_of(seq)
        for lo in range(2):
            for lane in range(2):
                lanes = slice(lane * LANE, (lane + 1) * LANE)
                value = left_tile(seq, lo, core, lane) + got_l[cx + lo, cy, cz, :, lanes].astype(F32)
                own_l[cx + lo, cy, cz, :, lanes] = value.astype(BF)
        return _

    lax.fori_loop(0, SEQ, pack_left, 0)
    pair_l = remote(sib_l, got_l, core_sems.at[0, 3], core_sems.at[1, 3], sibling)
    pair_l.start()
    for part in reduce_r:
        part.finish(0)
        part.start(1)
    outer(0)
    pair_l.wait()
    lax.fori_loop(0, SEQ, add_left, 0)
    for part in reduce_l:
        part.start(0)
    for part in reduce_r:
        part.finish(1)
        part.start(2)
    outer(1)
    for part in reduce_l:
        part.finish(0)
        part.start(1)
    outer(2)
    save.append(pltpu.make_async_copy(out, out_ref, stores.at[3]))
    save[3].start()
    for part in reduce_r:
        part.finish(2)
    for part in reduce_l:
        part.finish(1)
    for j in range(3):
        twisted.sent(j)
    for copy in save:
        copy.wait()


def layer(inputs, gate_values, kernel, grad_out, right, left):
    hbm = pl.BlockSpec(memory_space=pl.ANY)
    vmem = pl.BlockSpec(memory_space=pltpu.VMEM)
    rows = pltpu.VMEM((8, B, 384), BF)

    return pl.pallas_call(
        layer_kernel,
        out_shape=(
            jax.ShapeDtypeStruct((16, A, 384), BF),
            jax.ShapeDtypeStruct((8, B, 384), BF),
            jax.ShapeDtypeStruct((8, B, 384), BF),
            jax.ShapeDtypeStruct((8, B, 384), BF),
            jax.ShapeDtypeStruct((16, A), F32),
            jax.ShapeDtypeStruct((32, B), F32),
        ),
        in_specs=[hbm] * 6,
        out_specs=(hbm,) * 4 + (vmem,) * 2,
        scratch_shapes=[pltpu.VMEM((16, A, 384), BF)]
        + [rows] * 9
        + [
            pltpu.VMEM((H, B, B), BF),
            pltpu.VMEM((H, A, A), BF),
            pltpu.VMEM((3, H * B, LANE), F32),
            pltpu.VMEM((2, H * A, LANE), F32),
            pltpu.VMEM((4, 256, LANE), F32),
            pltpu.VMEM((4, 4, 4, 64, B), BF),
            pltpu.VMEM((4, 4, 4, 32, A), BF),
        ]
        + [pltpu.VMEM((4, 4, 4, 32, B), BF)] * 3
        + [pltpu.VMEM((3,) + (4,) * n + (32, B), BF) for n in (2, 1, 0)]
        + [pltpu.VMEM((4, 4, 4, 16, A), BF)] * 3
        + [
            pltpu.VMEM((3, 4, 4, 16, LANE), BF),
            pltpu.VMEM((15, 16, LANE), BF),
            pltpu.VMEM((15, 4, 16, LANE), BF),
            pltpu.VMEM((3, 16, LANE), BF),
            pltpu.SemaphoreType.DMA((7,)),
            pltpu.SemaphoreType.DMA((2, 3)),
            pltpu.SemaphoreType.DMA((4, 3, SEQ)),
            pltpu.SemaphoreType.DMA((4,)),
            pltpu.SemaphoreType.DMA((2, 4)),
            pltpu.SemaphoreType.DMA((2, 3, 3, 3)),
            pltpu.SemaphoreType.DMA((2, 3, 3, 3)),
            pltpu.SemaphoreType.DMA((4, 2, 4)),
            pltpu.SemaphoreType.DMA((4, 2, 16)),
        ],
        compiler_params=pltpu.CompilerParams(collective_id=0, has_side_effects=True, vmem_limit_bytes=60 << 20),
        name="layer",
    )(inputs, gate_values, kernel, grad_out, right, left)


def on_device(inputs, gate_values, kernel, grad_out, left_tiles, right_tiles):
    output, grad_inputs, grad_gates, grad_kernel, grad_left, grad_right = layer(
        inputs, gate_values, kernel, grad_out, right_tiles.reshape(32, B), left_tiles.reshape(16, A)
    )
    return (
        output,
        grad_inputs,
        grad_gates,
        grad_kernel,
        grad_left.reshape(2, H, A),
        grad_right.reshape(4, H, B),
    )


def solution(mesh):
    specs = (P("seq", None, "chan"),) * 4 + (P(("seq", "chan"), None, None),) * 2
    return jax.shard_map(on_device, mesh=mesh, in_specs=specs, out_specs=specs, check_vma=False)
```
